128 devices in a mesh: ctx: 16 (over z, x), doc: 8 (over y, core).
Axes of the slice: x: 4, y: 4, z: 4, core: 2. Of those that a mesh axis runs over, the one named last changes fastest.
Arguments:
- queries: bfloat16 [16384, 2048], P(('doc', 'ctx')), parts along dimension 0, may hold values from -4 to 4
- keys: bfloat16 [16384, 2048], P(('doc', 'ctx')), parts along dimension 0, may hold values from -4 to 4
- values: bfloat16 [16384, 2048], P(('doc', 'ctx')), parts along dimension 0, may hold values from -6 to 6
- outputs: bfloat16 [16384, 2048], P(('doc', 'ctx')), parts along dimension 0, may hold values from -2 to 2
- out_grad: bfloat16 [16384, 2048], P(('doc', 'ctx')), parts along dimension 0, may hold values from -2 to 2
- log_norm: bfloat16 [16, 16384], P(None, ('doc', 'ctx')), parts along dimension 1, may hold values from -0.5 to 12, as said below
Outputs:
- query_grad: bfloat16 [16384, 2048], P(('doc', 'ctx')), parts along dimension 0
- key_grad: bfloat16 [16384, 2048], P(('doc', 'ctx')), parts along dimension 0
- value_grad: bfloat16 [16384, 2048], P(('doc', 'ctx')), parts along dimension 0
The draws below stay inside these ranges and needn't reach their ends.
There are 8 independent parts, one for each index of `doc`. The reference program is written for one: setup_inputs(seed, part) draws one part's arguments, and reference() takes and returns one part's arrays. A program takes and returns all parts, laid end to end along the dimension named above; each array names one. Nothing has to cross between parts.
Inputs may be any that keep to these rules, and one draw needn't show every extreme that they name: log_norm[h, t] lies within 1 of log(t + 1) + 0.5, t counted from 0 within the document.
All inputs are finite; a program needn't handle non-finite values.
Results may differ from the reference program's by a relative error of at most 0.0062.
Values may be sent and summed in bfloat16 or wider, within the bound.
No kernel may reach another device: no remote copies, remote signals or barrier semaphores. Data moves between devices by JAX's collectives and lax.ppermute only.
A program may use at most 64 MiB of HBM per device.

```python
import jax
import jax.numpy as jnp
from jax import lax

HEADS = 16
HD = 128
D = 2048
TOKENS = 2048


def draw_log_norm(key, part):
    key = jax.random.fold_in(key, 7)
    position = jnp.arange(TOKENS, dtype=jnp.float32)
    noise = jax.random.uniform(key, (HEADS, TOKENS), jnp.float32, -0.5, 0.5)
    return (jnp.log(position + 1.0)[None, :] + 0.5 + noise).astype(jnp.bfloat16)


def block_scale(rng, extent, split, low, largest):
    loudness, own = 1.0, jax.random.fold_in(rng, 6)
    for dim, parts in split:
        steps = jnp.exp(jax.random.uniform(jax.random.fold_in(own, dim), (parts,), jnp.float32, low / len(split), largest / len(split)))
        loudness = loudness * jnp.repeat(steps, extent[dim] // parts).reshape([-1 if axis == dim else 1 for axis in range(len(extent))])
    return loudness


def centred(rng, shape, spread, bound, pieces=(), held_as=jnp.bfloat16):
    result = spread * jax.random.normal(rng, shape, jnp.float32)
    if pieces:
        result = result * block_scale(rng, shape, pieces, -0.22, 0.18)
    return jnp.clip(result, -bound, bound).astype(held_as)


def setup_inputs(seed: int = 0, part: int = 0) -> dict:
    splits = jax.random.split(jax.random.key(seed), 7)
    part_keys = jax.random.split(jax.random.fold_in(splits[6], part), 7)
    return {
        "queries": centred(part_keys[0], (TOKENS, D), 1.0, 4.0, ((0, 16),)),
        "keys": centred(part_keys[1], (TOKENS, D), 1.0, 4.0, ((0, 16),)),
        "values": centred(part_keys[2], (TOKENS, D), 1.0, 6.0, ((0, 16),)),
        "outputs": centred(part_keys[3], (TOKENS, D), 0.3, 2.0, ((0, 16),)),
        "out_grad": centred(part_keys[4], (TOKENS, D), 0.3, 2.0, ((0, 16),)),
        "log_norm": draw_log_norm(jax.random.fold_in(jax.random.fold_in(splits[6], part), 71), part),
    }


def reference(queries, keys, values, outputs, out_grad, log_norm):
    length = queries.shape[0]
    scale = HD ** -0.5
    delta = jnp.sum((out_grad.astype(jnp.float32) * outputs.astype(jnp.float32)).reshape(length, HEADS, HD), -1).T
    position = jnp.arange(length, dtype=jnp.int32)
    causal = position[None, :] <= position[:, None]

    def split_heads(array):
        return array.reshape(length, HEADS, HD).transpose(1, 0, 2)

    def one_head(items):
        query, key_rows, value_rows, grad_rows, lse_row, delta_row = items
        scores = jnp.dot(query, key_rows.T, preferred_element_type=jnp.float32) * scale
        probs = jnp.exp(jnp.where(causal, scores - lse_row.astype(jnp.float32)[:, None], -1e30))
        dprobs = jnp.dot(grad_rows, value_rows.T, preferred_element_type=jnp.float32)
        dscores = probs * (dprobs - delta_row[:, None])
        probs_low = probs.astype(jnp.bfloat16)
        dscores_low = dscores.astype(jnp.bfloat16)
        value_part = jnp.dot(probs_low.T, grad_rows, preferred_element_type=jnp.float32)
        key_part = jnp.dot(dscores_low.T, query, preferred_element_type=jnp.float32) * scale
        query_part = jnp.dot(dscores_low, key_rows, preferred_element_type=jnp.float32) * scale
        return query_part, key_part, value_part

    query_part, key_part, value_part = lax.map(one_head, (split_heads(queries), split_heads(keys), split_heads(values), split_heads(out_grad), log_norm, delta))

    def merge_heads(array):
        return array.transpose(1, 0, 2).reshape(length, HEADS * HD).astype(jnp.bfloat16)

    return merge_heads(query_part), merge_heads(key_part), merge_heads(value_part)
```

```python
import functools
import math

import jax
import jax.numpy as jnp
from jax import lax
from jax.experimental import pallas as pl
from jax.experimental.pallas import tpu as pltpu
from jax.sharding import PartitionSpec as P

HD = 128
SCALE = HD**-0.5
LOG2E = math.log2(math.e)
STATS = 16
TILE = 256
VMEM_LIMIT = 48 * 1024 * 1024

NT = (((1,), (1,)), ((), ()))
NN = (((1,), (0,)), ((), ()))


def dot(left, right, dims):
    return lax.dot_general(left, right, dims, preferred_element_type=jnp.float32)


def vmem_specs(count):
    return [pl.BlockSpec(memory_space=pltpu.VMEM)] * count


def pack_kernel(q_ref, k_ref, v_ref, o_ref, g_ref, lse_ref, send_ref):
    heads = send_ref.shape[0]
    rows = q_ref.shape[0]
    ones = jnp.ones((STATS, HD), jnp.bfloat16)
    which = lax.broadcasted_iota(jnp.int32, (STATS, rows), 0)
    for head in range(heads):
        cols = slice(head * HD, (head + 1) * HD)
        for place, ref in enumerate((q_ref, k_ref, v_ref, g_ref)):
            send_ref[head, place * rows : (place + 1) * rows, :] = ref[:, cols]
        product = g_ref[:, cols].astype(jnp.float32) * o_ref[:, cols].astype(jnp.float32)
        high = product.astype(jnp.bfloat16)
        low = (product - high.astype(jnp.float32)).astype(jnp.bfloat16)
        delta = dot(ones, high, NT) + dot(ones, low, NT)
        delta_high = delta.astype(jnp.bfloat16).astype(jnp.float32)
        delta_low = delta - delta_high
        lse = lse_ref[head : head + 1, :].astype(jnp.float32)
        stats = jnp.where(which == 0, lse, jnp.where(which == 1, delta_high, delta_low))
        send_ref[head, 4 * rows :, :] = stats.astype(jnp.bfloat16)


def head_kernel(x_ref, out_ref, p_ref, ds_ref, kt_ref, lse_ref, delta_ref):
    blocks = x_ref.shape[0]
    rows = HD
    tokens = blocks * rows

    def piece(place, start, count):
        part = x_ref[start // rows : (start + count) // rows, place * rows : (place + 1) * rows, :]
        return part.reshape(count, HD)

    def put(place, start, value):
        for step in range(value.shape[0] // rows):
            part = value[step * rows : (step + 1) * rows].astype(jnp.bfloat16)
            out_ref[start // rows + step, place * rows : (place + 1) * rows, :] = part

    for block in range(blocks):
        cols = slice(block * rows, (block + 1) * rows)
        stats = x_ref[block, 4 * rows :, :].astype(jnp.float32)
        lse_ref[:, cols] = jnp.broadcast_to(stats[0:1] * LOG2E, (8, rows))
        delta_ref[:, cols] = jnp.broadcast_to(stats[1:2] + stats[2:3], (8, rows))
        kt_ref[:, cols] = x_ref[block, rows : 2 * rows, :].T

    for key_start in range(0, tokens, TILE):
        keys = piece(1, key_start, TILE)
        values = piece(2, key_start, TILE)
        key_rows = slice(key_start, key_start + TILE)
        for start in range(key_start, tokens, TILE):
            cols = slice(start, start + TILE)
            scores = dot(keys, piece(0, start, TILE), NT)
            dprobs = dot(values, piece(3, start, TILE), NT)
            probs = jnp.exp2(scores * (SCALE * LOG2E) - lse_ref[0:1, cols])
            if start == key_start:
                key_pos = lax.broadcasted_iota(jnp.int32, (TILE, TILE), 0)
                query_pos = lax.broadcasted_iota(jnp.int32, (TILE, TILE), 1)
                probs = jnp.where(key_pos <= query_pos, probs, 0.0)
            dscores = probs * (dprobs - delta_ref[0:1, cols])
            p_ref[key_rows, cols] = probs.astype(jnp.bfloat16)
            ds_ref[key_rows, cols] = dscores.astype(jnp.bfloat16)
        count = tokens - key_start
        put(1, key_start, dot(ds_ref[key_rows, key_start:], piece(0, key_start, count), NN) * SCALE)
        put(2, key_start, dot(p_ref[key_rows, key_start:], piece(3, key_start, count), NN))
    for start in range(0, tokens, TILE):
        stop = start + TILE
        query_grad = dot(kt_ref[:, :stop], ds_ref[:stop, start:stop], NN)
        put(0, start, query_grad.T * SCALE)


def unpack_kernel(recv_ref, dq_ref, dk_ref, dv_ref):
    rows = dq_ref.shape[0]
    for head in range(recv_ref.shape[0]):
        cols = slice(head * HD, (head + 1) * HD)
        for place, ref in enumerate((dq_ref, dk_ref, dv_ref)):
            ref[:, cols] = recv_ref[head, place * rows : (place + 1) * rows, :]


def call(kernel, ins, outs, scratch=()):
    return pl.pallas_call(
        kernel,
        out_shape=outs,
        in_specs=vmem_specs(ins),
        out_specs=jax.tree.map(lambda _: vmem_specs(1)[0], outs),
        scratch_shapes=scratch,
        compiler_params=pltpu.CompilerParams(vmem_limit_bytes=VMEM_LIMIT),
    )


def local(queries, keys, values, outputs, out_grad, log_norm):
    rows, width = queries.shape
    heads = width // HD
    tokens = rows * lax.axis_size("ctx")
    bf16 = functools.partial(jax.ShapeDtypeStruct, dtype=jnp.bfloat16)
    with jax.named_scope("pack"):
        send = call(pack_kernel, 6, bf16((heads, 4 * rows + STATS, HD)))(
            queries, keys, values, outputs, out_grad, log_norm
        )
    with jax.named_scope("to_heads"):
        x = lax.all_to_all(send, "ctx", 0, 0, tiled=True)
    with jax.named_scope("head_grads"):
        scratch = (
            pltpu.VMEM((tokens, tokens), jnp.bfloat16),
            pltpu.VMEM((tokens, tokens), jnp.bfloat16),
            pltpu.VMEM((HD, tokens), jnp.bfloat16),
            pltpu.VMEM((8, tokens), jnp.float32),
            pltpu.VMEM((8, tokens), jnp.float32),
        )
        grads = call(head_kernel, 1, bf16((heads, 3 * rows, HD)), scratch)(x)
    with jax.named_scope("to_tokens"):
        back = lax.all_to_all(grads, "ctx", 0, 0, tiled=True)
    with jax.named_scope("unpack"):
        return call(unpack_kernel, 1, (bf16((rows, width)),) * 3)(back)


def solution(mesh):
    tokens = P(("doc", "ctx"), None)
    in_specs = (tokens,) * 5 + (P(None, ("doc", "ctx")),)
    return jax.shard_map(
        local, mesh=mesh, in_specs=in_specs, out_specs=(tokens,) * 3, check_vma=False
    )
```

```python
import functools
import math

import jax
import jax.numpy as jnp
from jax import lax
from jax.experimental import pallas as pl
from jax.experimental.pallas import tpu as pltpu
from jax.sharding import PartitionSpec as P

HD = 128
SCALE = HD**-0.5
LOG2E = math.log2(math.e)
STATS = 16
TILE = 256
VMEM_LIMIT = 48 * 1024 * 1024

NT = (((1,), (1,)), ((), ()))
NN = (((1,), (0,)), ((), ()))


def dot(left, right, dims):
    return lax.dot_general(left, right, dims, preferred_element_type=jnp.float32)


def pack_kernel(q_ref, k_ref, v_ref, o_ref, g_ref, lse_ref, send_ref, o_buf, lse_buf, sems):
    heads = send_ref.shape[0]
    rows = q_ref.shape[0]
    own = (
        pltpu.make_async_copy(o_ref, o_buf, sems.at[4]),
        pltpu.make_async_copy(lse_ref, lse_buf, sems.at[5]),
    )
    for copy in own:
        copy.start()
    sources = (q_ref, k_ref, v_ref, g_ref)
    for place in (3, 0, 1, 2):
        for head in range(heads):
            pltpu.make_async_copy(
                sources[place].at[:, head * HD : (head + 1) * HD],
                send_ref.at[head, place * rows : (place + 1) * rows, :],
                sems.at[place],
            ).start()
    for copy in own:
        copy.wait()
    pltpu.make_async_copy(g_ref, g_ref, sems.at[3]).wait()
    ones = jnp.ones((STATS, HD), jnp.bfloat16)
    which = lax.broadcasted_iota(jnp.int32, (STATS, rows), 0)
    for head in range(heads):
        cols = slice(head * HD, (head + 1) * HD)
        grads = send_ref[head, 3 * rows : 4 * rows, :]
        product = grads.astype(jnp.float32) * o_buf[:, cols].astype(jnp.float32)
        high = product.astype(jnp.bfloat16)
        low = (product - high.astype(jnp.float32)).astype(jnp.bfloat16)
        delta = dot(ones, high, NT) + dot(ones, low, NT)
        delta_high = delta.astype(jnp.bfloat16).astype(jnp.float32)
        delta_low = delta - delta_high
        lse = lse_buf[head : head + 1, :].astype(jnp.float32)
        stats = jnp.where(which == 0, lse, jnp.where(which == 1, delta_high, delta_low))
        send_ref[head, 4 * rows :, :] = stats.astype(jnp.bfloat16)
    for place in range(3):
        pltpu.make_async_copy(sources[place], sources[place], sems.at[place]).wait()


def head_kernel(x_ref, out_ref, p_ref, ds_ref, kt_ref, lse_ref, delta_ref):
    blocks = x_ref.shape[0]
    rows = HD
    tokens = blocks * rows

    def piece(place, start, count):
        part = x_ref[start // rows : (start + count) // rows, place * rows : (place + 1) * rows, :]
        return part.reshape(count, HD)

    def put(place, start, value):
        for step in range(value.shape[0] // rows):
            part = value[step * rows : (step + 1) * rows].astype(jnp.bfloat16)
            out_ref[start // rows + step, place * rows : (place + 1) * rows, :] = part

    for block in range(blocks):
        cols = slice(block * rows, (block + 1) * rows)
        stats = x_ref[block, 4 * rows :, :].astype(jnp.float32)
        lse_ref[:, cols] = jnp.broadcast_to(stats[0:1] * LOG2E, (8, rows))
        delta_ref[:, cols] = jnp.broadcast_to(stats[1:2] + stats[2:3], (8, rows))
        kt_ref[:, cols] = x_ref[block, rows : 2 * rows, :].T

    for key_start in range(0, tokens, TILE):
        keys = piece(1, key_start, TILE)
        values = piece(2, key_start, TILE)
        key_rows = slice(key_start, key_start + TILE)
        for start in range(key_start, tokens, TILE):
            cols = slice(start, start + TILE)
            scores = dot(keys, piece(0, start, TILE), NT)
            dprobs = dot(values, piece(3, start, TILE), NT)
            probs = jnp.exp2(scores * (SCALE * LOG2E) - lse_ref[0:1, cols])
            if start == key_start:
                key_pos = lax.broadcasted_iota(jnp.int32, (TILE, TILE), 0)
                query_pos = lax.broadcasted_iota(jnp.int32, (TILE, TILE), 1)
                probs = jnp.where(key_pos <= query_pos, probs, 0.0)
            dscores = probs * (dprobs - delta_ref[0:1, cols])
            p_ref[key_rows, cols] = probs.astype(jnp.bfloat16)
            ds_ref[key_rows, cols] = dscores.astype(jnp.bfloat16)
        count = tokens - key_start
        put(1, key_start, dot(ds_ref[key_rows, key_start:], piece(0, key_start, count), NN) * SCALE)
        put(2, key_start, dot(p_ref[key_rows, key_start:], piece(3, key_start, count), NN))
    for start in range(0, tokens, TILE):
        stop = start + TILE
        query_grad = dot(kt_ref[:, :stop], ds_ref[:stop, start:stop], NN)
        put(0, start, query_grad.T * SCALE)


def unpack_kernel(recv_ref, dq_ref, dk_ref, dv_ref, sems):
    rows = dq_ref.shape[0]
    outs = (dq_ref, dk_ref, dv_ref)
    for place, ref in enumerate(outs):
        for head in range(recv_ref.shape[0]):
            pltpu.make_async_copy(
                recv_ref.at[head, place * rows : (place + 1) * rows, :],
                ref.at[:, head * HD : (head + 1) * HD],
                sems.at[place],
            ).start()
    for place, ref in enumerate(outs):
        pltpu.make_async_copy(ref, ref, sems.at[place]).wait()


IN_HBM = pl.BlockSpec(memory_space=pl.ANY)
IN_VMEM = pl.BlockSpec(memory_space=pltpu.VMEM)


def call(kernel, ins, outs, out_specs, scratch):
    return pl.pallas_call(
        kernel,
        out_shape=outs,
        in_specs=ins,
        out_specs=out_specs,
        scratch_shapes=scratch,
        compiler_params=pltpu.CompilerParams(vmem_limit_bytes=VMEM_LIMIT),
    )


def local(queries, keys, values, outputs, out_grad, log_norm):
    rows, width = queries.shape
    heads = width // HD
    tokens = rows * lax.axis_size("ctx")
    bf16 = functools.partial(jax.ShapeDtypeStruct, dtype=jnp.bfloat16)
    with jax.named_scope("pack"):
        scratch = (
            pltpu.VMEM((rows, width), jnp.bfloat16),
            pltpu.VMEM((heads, rows), jnp.bfloat16),
            pltpu.SemaphoreType.DMA((6,)),
        )
        shape = bf16((heads, 4 * rows + STATS, HD))
        send = call(pack_kernel, [IN_HBM] * 6, shape, IN_VMEM, scratch)(
            queries, keys, values, outputs, out_grad, log_norm
        )
    with jax.named_scope("to_heads"):
        x = lax.all_to_all(send, "ctx", 0, 0, tiled=True)
    with jax.named_scope("head_grads"):
        scratch = (
            pltpu.VMEM((tokens, tokens), jnp.bfloat16),
            pltpu.VMEM((tokens, tokens), jnp.bfloat16),
            pltpu.VMEM((HD, tokens), jnp.bfloat16),
            pltpu.VMEM((8, tokens), jnp.float32),
            pltpu.VMEM((8, tokens), jnp.float32),
        )
        shape = bf16((heads, 3 * rows, HD))
        grads = call(head_kernel, [IN_VMEM], shape, IN_VMEM, scratch)(x)
    with jax.named_scope("to_tokens"):
        back = lax.all_to_all(grads, "ctx", 0, 0, tiled=True)
    with jax.named_scope("unpack"):
        shapes = (bf16((rows, width)),) * 3
        scratch = (pltpu.SemaphoreType.DMA((3,)),)
        return call(unpack_kernel, [IN_VMEM], shapes, (IN_HBM,) * 3, scratch)(back)


def solution(mesh):
    tokens = P(("doc", "ctx"), None)
    in_specs = (tokens,) * 5 + (P(None, ("doc", "ctx")),)
    return jax.shard_map(
        local, mesh=mesh, in_specs=in_specs, out_specs=(tokens,) * 3, check_vma=False
    )
```

```python
import functools
import math

import jax
import jax.numpy as jnp
from jax import lax
from jax.experimental import pallas as pl
from jax.experimental.pallas import tpu as pltpu
from jax.sharding import PartitionSpec as P

HD = 128
SCALE = HD**-0.5
LOG2E = math.log2(math.e)
STATS = 16
TILE = 256
HEAD_LIMIT = 48 * 1024 * 1024
PACK_LIMIT = 60 * 1024 * 1024

NT = (((1,), (1,)), ((), ()))
NN = (((1,), (0,)), ((), ()))

IN_HBM = pl.BlockSpec(memory_space=pltpu.HBM)
IN_VMEM = pl.BlockSpec(memory_space=pltpu.VMEM)


def dot(left, right, dims):
    return lax.dot_general(left, right, dims, preferred_element_type=jnp.float32)


def row_stats(grads, outs, lse):
    product = grads.astype(jnp.float32) * outs.astype(jnp.float32)
    high = product.astype(jnp.bfloat16)
    low = (product - high.astype(jnp.float32)).astype(jnp.bfloat16)
    ones = jnp.ones((STATS, HD), jnp.bfloat16)
    delta = dot(ones, high, NT) + dot(ones, low, NT)
    delta_high = delta.astype(jnp.bfloat16).astype(jnp.float32)
    which = lax.broadcasted_iota(jnp.int32, delta.shape, 0)
    stats = jnp.where(which == 1, delta_high, delta - delta_high)
    return jnp.where(which == 0, lse.astype(jnp.float32), stats).astype(jnp.bfloat16)


def pack_kernel(count, stats, *refs):
    total = max((count, *(place + 1 for place in stats)))
    sources, send_ref, held = refs[:total], refs[total], refs[total + 1 : 2 * total + 1]
    image, in_sems, out_sems = refs[2 * total + 1 :]
    heads = send_ref.shape[0]
    rows = sources[0].shape[0]

    def out(place):
        part = slice(place * rows, (place + 1) * rows if place < count else send_ref.shape[1])
        return pltpu.make_async_copy(
            image.at[:, part, :], send_ref.at[:, part, :], out_sems.at[place]
        )

    copies = [
        pltpu.make_async_copy(source, buffer, in_sems.at[place])
        for place, (source, buffer) in enumerate(zip(sources, held, strict=True))
    ]
    for copy in copies:
        copy.start()
    for place in range(count):
        copies[place].wait()
        for head in range(heads):
            image[head, place * rows : (place + 1) * rows, :] = held[place][
                :, head * HD : (head + 1) * HD
            ]
        out(place).start()
    if stats:
        for place in range(count, total):
            copies[place].wait()
        grads, outs, lse = (held[place] for place in stats)
        for head in range(heads):
            cols = slice(head * HD, (head + 1) * HD)
            image[head, count * rows :, :] = row_stats(
                grads[:, cols], outs[:, cols], lse[head : head + 1, :]
            )
        out(count).start()
    for place in range(count + bool(stats)):
        out(place).wait()


def head_kernel(layout, count, *refs):
    received, refs = refs[:count], refs[count:]
    out_ref, p_ref, ds_ref, kt_ref, lse_ref, delta_ref = refs
    blocks = out_ref.shape[0]
    rows = out_ref.shape[1] // 3
    tokens = blocks * rows

    def piece(name, start, count):
        which, at = layout[name]
        part = received[which][start // rows : (start + count) // rows, at : at + rows, :]
        return part.reshape(count, HD)

    def put(place, start, value):
        for step in range(value.shape[0] // rows):
            part = value[step * rows : (step + 1) * rows].astype(jnp.bfloat16)
            out_ref[start // rows + step, place * rows : (place + 1) * rows, :] = part

    for block in range(blocks):
        cols = slice(block * rows, (block + 1) * rows)
        which, at = layout["stats"]
        stats = received[which][block, at : at + STATS, :].astype(jnp.float32)
        lse_ref[:, cols] = jnp.broadcast_to(stats[0:1] * LOG2E, (8, rows))
        delta_ref[:, cols] = jnp.broadcast_to(stats[1:2] + stats[2:3], (8, rows))
        kt_ref[:, cols] = piece("k", block * rows, rows).T

    for key_start in range(0, tokens, TILE):
        keys = piece("k", key_start, TILE)
        values = piece("v", key_start, TILE)
        key_rows = slice(key_start, key_start + TILE)
        for start in range(key_start, tokens, TILE):
            cols = slice(start, start + TILE)
            scores = dot(keys, piece("q", start, TILE), NT)
            dprobs = dot(values, piece("g", start, TILE), NT)
            probs = jnp.exp2(scores * (SCALE * LOG2E) - lse_ref[0:1, cols])
            if start == key_start:
                key_pos = lax.broadcasted_iota(jnp.int32, (TILE, TILE), 0)
                query_pos = lax.broadcasted_iota(jnp.int32, (TILE, TILE), 1)
                probs = jnp.where(key_pos <= query_pos, probs, 0.0)
            dscores = probs * (dprobs - delta_ref[0:1, cols])
            p_ref[key_rows, cols] = probs.astype(jnp.bfloat16)
            ds_ref[key_rows, cols] = dscores.astype(jnp.bfloat16)
        rest = tokens - key_start
        put(1, key_start, dot(ds_ref[key_rows, key_start:], piece("q", key_start, rest), NN) * SCALE)
        put(2, key_start, dot(p_ref[key_rows, key_start:], piece("g", key_start, rest), NN))
    for start in range(0, tokens, TILE):
        stop = start + TILE
        query_grad = dot(kt_ref[:, :stop], ds_ref[:stop, start:stop], NN)
        put(0, start, query_grad.T * SCALE)


def unpack_kernel(recv_ref, dq_ref, dk_ref, dv_ref, sems):
    rows = dq_ref.shape[0]
    outs = (dq_ref, dk_ref, dv_ref)
    for place, ref in enumerate(outs):
        for head in range(recv_ref.shape[0]):
            pltpu.make_async_copy(
                recv_ref.at[head, place * rows : (place + 1) * rows, :],
                ref.at[:, head * HD : (head + 1) * HD],
                sems.at[place],
            ).start()
    for place, ref in enumerate(outs):
        pltpu.make_async_copy(ref, ref, sems.at[place]).wait()


def bf16(*shape):
    return jax.ShapeDtypeStruct(shape, jnp.bfloat16)


def pack(operands, count, stats=()):
    rows, width = operands[0].shape
    shape = bf16(width // HD, count * rows + bool(stats) * STATS, HD)
    scratch = [pltpu.VMEM(operand.shape, operand.dtype) for operand in operands]
    scratch += [
        pltpu.VMEM(shape.shape, shape.dtype),
        pltpu.SemaphoreType.DMA((len(operands),)),
        pltpu.SemaphoreType.DMA((count + bool(stats),)),
    ]
    with jax.named_scope("pack"):
        return pl.pallas_call(
            functools.partial(pack_kernel, count, stats),
            out_shape=shape,
            in_specs=[IN_HBM] * len(operands),
            out_specs=IN_HBM,
            scratch_shapes=scratch,
            compiler_params=pltpu.CompilerParams(vmem_limit_bytes=PACK_LIMIT),
        )(*operands)


def exchange(chunks):
    with jax.named_scope("exchange"):
        return lax.all_to_all(chunks, "ctx", 0, 0, tiled=True)


def head_grads(layout, received, rows):
    tokens = received[0].shape[0] * rows
    with jax.named_scope("head_grads"):
        return pl.pallas_call(
            functools.partial(head_kernel, layout, len(received)),
            out_shape=bf16(received[0].shape[0], 3 * rows, HD),
            in_specs=[IN_VMEM] * len(received),
            out_specs=IN_VMEM,
            scratch_shapes=(
                pltpu.VMEM((tokens, tokens), jnp.bfloat16),
                pltpu.VMEM((tokens, tokens), jnp.bfloat16),
                pltpu.VMEM((HD, tokens), jnp.bfloat16),
                pltpu.VMEM((8, tokens), jnp.float32),
                pltpu.VMEM((8, tokens), jnp.float32),
            ),
            compiler_params=pltpu.CompilerParams(vmem_limit_bytes=HEAD_LIMIT),
        )(*received)


def unpack(received, rows, width):
    with jax.named_scope("unpack"):
        return pl.pallas_call(
            unpack_kernel,
            out_shape=(bf16(rows, width),) * 3,
            in_specs=[IN_VMEM],
            out_specs=(IN_HBM,) * 3,
            scratch_shapes=(pltpu.SemaphoreType.DMA((3,)),),
            compiler_params=pltpu.CompilerParams(vmem_limit_bytes=HEAD_LIMIT),
        )(received)


def local(queries, keys, values, outputs, out_grad, log_norm):
    rows, width = queries.shape

    def at_once():
        everything = (queries, keys, values, out_grad, outputs, log_norm)
        received = exchange(pack(everything, 4, (3, 4, 5)))
        layout = {"q": (0, 0), "k": (0, rows), "v": (0, 2 * rows), "g": (0, 3 * rows), "stats": (0, 4 * rows)}
        return head_grads(layout, (received,), rows)

    def in_two():
        first = exchange(pack((out_grad, outputs, log_norm), 0, (0, 1, 2)))
        second = exchange(pack((queries, keys, values, out_grad), 4))
        layout = {"q": (1, 0), "k": (1, rows), "v": (1, 2 * rows), "g": (1, 3 * rows), "stats": (0, 0)}
        return head_grads(layout, (first, second), rows)

    grads = lax.cond(lax.axis_index("doc") % 2 == 0, in_two, at_once)
    return unpack(exchange(grads), rows, width)


def solution(mesh):
    tokens = P(("doc", "ctx"), None)
    in_specs = (tokens,) * 5 + (P(None, ("doc", "ctx")),)
    return jax.shard_map(
        local, mesh=mesh, in_specs=in_specs, out_specs=(tokens,) * 3, check_vma=False
    )
```

```python
import functools
import math

import jax
import jax.numpy as jnp
from jax import lax
from jax.experimental import pallas as pl
from jax.experimental.pallas import tpu as pltpu
from jax.sharding import PartitionSpec as P

HD = 128
SCALE = HD**-0.5
LOG2E = math.log2(math.e)
STATS = 16
KERNEL_LIMIT = 32 * 1024 * 1024

NT = (((1,), (1,)), ((), ()))
NN = (((1,), (0,)), ((), ()))
TN = (((0,), (0,)), ((), ()))

IN_HBM = pl.BlockSpec(memory_space=pltpu.HBM)
IN_VMEM = pl.BlockSpec(memory_space=pltpu.VMEM)


def dot(left, right, dims):
    return lax.dot_general(left, right, dims, preferred_element_type=jnp.float32)


def row_stats(grads, outs, lse):
    product = (grads.astype(jnp.float32) * outs.astype(jnp.float32)).T
    delta = jnp.sum(product, axis=0, keepdims=True)
    delta_high = delta.astype(jnp.bfloat16).astype(jnp.float32)
    which = lax.broadcasted_iota(jnp.int32, (STATS, delta.shape[1]), 0)
    stats = jnp.where(which == 1, delta_high, delta - delta_high)
    return jnp.where(which == 0, lse.astype(jnp.float32), stats).astype(jnp.bfloat16)


def score_grads(scores, dprobs, stats):
    probs = jnp.exp2(scores * (SCALE * LOG2E) - stats[0:1] * LOG2E)
    return probs, dprobs - stats[1:2] - stats[2:3]


def fetch(sources, held, sems):
    copies = [
        pltpu.make_async_copy(source, buffer, sems.at[place])
        for place, (source, buffer) in enumerate(zip(sources, held, strict=True))
    ]
    for copy in copies:
        copy.start()
    return copies


def pack_kernel(*refs):
    sources, send_ref, held, sems = refs[:6], refs[6], refs[7:13], refs[13]
    heads = send_ref.shape[0]
    rows = sources[0].shape[0]
    copies = fetch(sources, held, sems)
    for place in range(4):
        copies[place].wait()
        for head in range(heads):
            cols = slice(head * HD, (head + 1) * HD)
            send_ref[head, place * rows : (place + 1) * rows, :] = held[place][:, cols]
    copies[4].wait()
    copies[5].wait()
    for head in range(heads):
        cols = slice(head * HD, (head + 1) * HD)
        send_ref[head, 4 * rows :, :] = row_stats(
            held[3][:, cols], held[4][:, cols], held[5][head : head + 1, :]
        )


def repack_kernel(*refs):
    sources, stats_ref, send_ref, held, sems = refs[:4], refs[4], refs[5], refs[6:10], refs[10]
    heads = send_ref.shape[0]
    rows = sources[0].shape[0]
    copies = fetch(sources, held, sems)
    send_ref[:, 4 * rows :, :] = stats_ref[...]
    for place in range(4):
        copies[place].wait()
        for head in range(heads):
            cols = slice(head * HD, (head + 1) * HD)
            send_ref[head, place * rows : (place + 1) * rows, :] = held[place][:, cols]


def near_head(query, keys, values, grads, stats):
    scores = dot(keys, query, NT)
    dprobs = dot(values, grads, NT)
    probs, centred = score_grads(scores, dprobs, stats.astype(jnp.float32))
    key_pos = lax.broadcasted_iota(jnp.int32, probs.shape, 0)
    query_pos = lax.broadcasted_iota(jnp.int32, probs.shape, 1)
    probs = jnp.where(key_pos <= query_pos, probs, 0.0)
    dscores = (probs * centred).astype(jnp.bfloat16)
    query_grad = dot(dscores, keys, TN) * SCALE
    key_grad = dot(dscores, query, NN) * SCALE
    return query_grad, key_grad, dot(probs.astype(jnp.bfloat16), grads, NN)


def near_kernel(*refs):
    sources, outs, stats_ref, held, sems = refs[:6], refs[6:9], refs[9], refs[10:16], refs[16]
    for copy in fetch(sources, held, sems):
        copy.wait()
    for head in range(stats_ref.shape[0]):
        cols = slice(head * HD, (head + 1) * HD)
        parts = [held[place][:, cols] for place in range(4)]
        stats = row_stats(parts[3], held[4][:, cols], held[5][head : head + 1, :])
        stats_ref[head] = stats
        for ref, term in zip(outs, near_head(*parts, stats), strict=True):
            ref[:, cols] = term


class Head:
    def __init__(self, x_ref, out_ref, p_ref, ds_ref, kt_ref, stats_ref):
        self.x, self.out, self.p, self.ds, self.kt, self.stats = x_ref, out_ref, p_ref, ds_ref, kt_ref, stats_ref
        self.rows = out_ref.shape[1] // 3
        self.tokens = x_ref.shape[0] * self.rows
        for start in range(0, self.tokens, self.rows):
            cols = slice(start, start + self.rows)
            stats = x_ref[start // self.rows, 4 * self.rows :, :].astype(jnp.float32)
            stats_ref[0:1, cols] = stats[0:1] * LOG2E
            stats_ref[1:2, cols] = stats[1:2] + stats[2:3]
            kt_ref[:, cols] = self.piece(1, start, self.rows).T

    def piece(self, place, start, count):
        rows = self.rows
        blocks = slice(start // rows, (start + count) // rows)
        return self.x[blocks, place * rows : (place + 1) * rows, :].reshape(count, HD)

    def put(self, place, start, value):
        rows = self.rows
        for step in range(value.shape[0] // rows):
            part = value[step * rows : (step + 1) * rows].astype(jnp.bfloat16)
            self.out[start // rows + step, place * rows : (place + 1) * rows, :] = part

    def tile(self, keys, values, key_start, start, count, masked=False):
        key_rows, cols = slice(key_start, key_start + keys.shape[0]), slice(start, start + count)
        scores = dot(keys, self.piece(0, start, count), NT)
        dprobs = dot(values, self.piece(3, start, count), NT)
        probs = jnp.exp2(scores * (SCALE * LOG2E) - self.stats[0:1, cols])
        if masked:
            key_pos = lax.broadcasted_iota(jnp.int32, probs.shape, 0)
            query_pos = lax.broadcasted_iota(jnp.int32, probs.shape, 1)
            probs = jnp.where(key_pos <= query_pos, probs, 0.0)
        dscores = probs * (dprobs - self.stats[1:2, cols])
        self.p[key_rows, cols] = probs.astype(jnp.bfloat16)
        self.ds[key_rows, cols] = dscores.astype(jnp.bfloat16)


def whole_head_kernel(*refs):
    head = Head(*refs)
    step, tokens = 2 * head.rows, head.tokens
    for first in range(0, tokens, step):
        keys, values = head.piece(1, first, step), head.piece(2, first, step)
        for start in range(first, tokens, step):
            head.tile(keys, values, first, start, step, masked=start == first)
        rest, part = tokens - first, slice(first, first + step)
        head.put(1, first, dot(head.ds[part, first:], head.piece(0, first, rest), NN) * SCALE)
        head.put(2, first, dot(head.p[part, first:], head.piece(3, first, rest), NN))
    for first in range(0, tokens, step):
        stop = first + step
        head.put(0, first, dot(head.kt[:, :stop], head.ds[:stop, first:stop], NN).T * SCALE)


def far_head_kernel(*refs):
    head = Head(*refs)
    rows, tokens = head.rows, head.tokens
    step = 2 * rows
    for first in range(0, tokens, step):
        second, stop = first + rows, first + step
        keys, values = head.piece(1, first, step), head.piece(2, first, step)
        head.tile(keys[:rows], values[:rows], first, second, rows)
        for start in range(stop, tokens, step):
            head.tile(keys, values, first, start, step)
        for place, source, factor, ref in ((1, 0, SCALE, head.ds), (2, 3, 1.0, head.p)):
            total = dot(ref[first:second, second:stop], head.piece(source, second, rows), NN)
            after = jnp.zeros_like(total)
            if stop < tokens:
                far = dot(ref[first:stop, stop:], head.piece(source, stop, tokens - stop), NN)
                total, after = total + far[:rows], far[rows:]
            head.put(place, first, total * factor)
            head.put(place, second, after * factor)
    for first in range(0, tokens, step):
        second, stop = first + rows, first + step
        total = dot(head.kt[:, first:second], head.ds[first:second, second:stop], NN)
        before = jnp.zeros_like(total)
        if first > 0:
            far = dot(head.kt[:, :first], head.ds[:first, first:stop], NN)
            before, total = far[:, :rows], total + far[:, rows:]
        head.put(0, first, before.T * SCALE)
        head.put(0, second, total.T * SCALE)


def unpack_kernel(recv_ref, *refs):
    outs, sems = refs[:3], refs[3]
    rows = outs[0].shape[0]
    for place, ref in enumerate(outs):
        for head in range(recv_ref.shape[0]):
            pltpu.make_async_copy(
                recv_ref.at[head, place * rows : (place + 1) * rows, :],
                ref.at[:, head * HD : (head + 1) * HD],
                sems.at[place],
            ).start()
    for place, ref in enumerate(outs):
        pltpu.make_async_copy(ref, ref, sems.at[place]).wait()


def unpack_add_kernel(recv_ref, *refs):
    near, outs, sums, sems = refs[:3], refs[3:6], refs[6:9], refs[9]
    rows = outs[0].shape[0]
    copies = []
    for place, (part, buffer, ref) in enumerate(zip(near, sums, outs, strict=True)):
        for head in range(recv_ref.shape[0]):
            cols = slice(head * HD, (head + 1) * HD)
            far = recv_ref[head, place * rows : (place + 1) * rows, :].astype(jnp.float32)
            buffer[:, cols] = (far + part[:, cols]).astype(jnp.bfloat16)
        copies.append(pltpu.make_async_copy(buffer, ref, sems.at[place]))
        copies[-1].start()
    for copy in copies:
        copy.wait()


def bf16(*shape):
    return jax.ShapeDtypeStruct(shape, jnp.bfloat16)


def f32(*shape):
    return jax.ShapeDtypeStruct(shape, jnp.float32)


def call(kernel, name, in_specs, out_specs, out_shape, scratch):
    def run(*operands):
        operands = [
            pltpu.with_memory_space_constraint(operand, pltpu.HBM) if spec is IN_HBM else operand
            for spec, operand in zip(in_specs, operands, strict=True)
        ]
        with jax.named_scope(name):
            return pl.pallas_call(
                kernel,
                out_shape=out_shape,
                in_specs=in_specs,
                out_specs=out_specs,
                scratch_shapes=scratch,
                compiler_params=pltpu.CompilerParams(vmem_limit_bytes=KERNEL_LIMIT),
            )(*operands)

    return run


def exchange(chunks):
    with jax.named_scope("exchange"):
        return lax.all_to_all(chunks, "ctx", 0, 0, tiled=True)


def local(*arguments):
    queries, keys, values, outputs, out_grad, log_norm = arguments
    rows, width = queries.shape
    heads = width // HD
    tokens = rows * lax.axis_size("ctx")
    everything = (queries, keys, values, out_grad, outputs, log_norm)
    held = [pltpu.VMEM(operand.shape, operand.dtype) for operand in everything]
    chunk = bf16(heads, 4 * rows + STATS, HD)
    result = (bf16(rows, width),) * 3
    copies = pltpu.SemaphoreType.DMA

    def head_grads(kernel, x):
        scratch = (
            pltpu.VMEM((tokens, tokens), jnp.bfloat16),
            pltpu.VMEM((tokens, tokens), jnp.bfloat16),
            pltpu.VMEM((HD, tokens), jnp.bfloat16),
            pltpu.VMEM((8, tokens), jnp.float32),
        )
        shape = bf16(heads, 3 * rows, HD)
        return call(kernel, "head_grads", [IN_VMEM], IN_VMEM, shape, scratch)(x)

    def goes_first():
        pack = call(pack_kernel, "pack", [IN_HBM] * 6, IN_VMEM, chunk, (*held, copies((6,))))
        back = exchange(head_grads(whole_head_kernel, exchange(pack(*everything))))
        unpack = call(unpack_kernel, "unpack", [IN_VMEM], (IN_HBM,) * 3, result, (copies((3,)),))
        return unpack(back)

    def goes_second():
        shapes = (*(f32(rows, width),) * 3, bf16(heads, STATS, HD))
        near = call(near_kernel, "near", [IN_HBM] * 6, (IN_VMEM,) * 4, shapes, (*held, copies((6,))))
        *terms, stats = near(*everything)
        specs, scratch = [IN_HBM] * 4 + [IN_VMEM], (*held[:4], copies((4,)))
        pack = call(repack_kernel, "pack", specs, IN_VMEM, chunk, scratch)
        back = exchange(head_grads(far_head_kernel, exchange(pack(*everything[:4], stats))))
        scratch = (*(pltpu.VMEM((rows, width), jnp.bfloat16),) * 3, copies((3,)))
        unpack = call(unpack_add_kernel, "unpack", [IN_VMEM] * 4, (IN_HBM,) * 3, result, scratch)
        return unpack(back, *terms)

    return lax.cond(lax.axis_index("doc") % 2 == 1, goes_first, goes_second)


def solution(mesh):
    tokens = P(("doc", "ctx"), None)
    in_specs = (tokens,) * 5 + (P(None, ("doc", "ctx")),)
    return jax.shard_map(
        local, mesh=mesh, in_specs=in_specs, out_specs=(tokens,) * 3, check_vma=False
    )
```

```python
import functools
import math

import jax
import jax.numpy as jnp
from jax import lax
from jax.experimental import pallas as pl
from jax.experimental.pallas import tpu as pltpu
from jax.sharding import PartitionSpec as P

HD = 128
SCALE = HD**-0.5
LOG2E = math.log2(math.e)
STATS = 16
KERNEL_LIMIT = 32 * 1024 * 1024

NT = (((1,), (1,)), ((), ()))
NN = (((1,), (0,)), ((), ()))
TN = (((0,), (0,)), ((), ()))

IN_HBM = pl.BlockSpec(memory_space=pltpu.HBM)
IN_VMEM = pl.BlockSpec(memory_space=pltpu.VMEM)


def dot(left, right, dims):
    return lax.dot_general(left, right, dims, preferred_element_type=jnp.float32)


def row_stats(grads, outs, lse):
    product = (grads.astype(jnp.float32) * outs.astype(jnp.float32)).T
    delta = jnp.sum(product, axis=0, keepdims=True)
    delta_high = delta.astype(jnp.bfloat16).astype(jnp.float32)
    which = lax.broadcasted_iota(jnp.int32, (STATS, delta.shape[1]), 0)
    stats = jnp.where(which == 1, delta_high, delta - delta_high)
    return jnp.where(which == 0, lse.astype(jnp.float32), stats).astype(jnp.bfloat16)


def score_grads(scores, dprobs, stats):
    probs = jnp.exp2(scores * (SCALE * LOG2E) - stats[0:1] * LOG2E)
    return probs, dprobs - stats[1:2] - stats[2:3]


def fetch(sources, held, sems, order):
    copies = [
        pltpu.make_async_copy(source, buffer, sems.at[place])
        for place, (source, buffer) in enumerate(zip(sources, held, strict=True))
    ]
    for place in order:
        copies[place].start()
    return copies


def pack_kernel(*refs):
    sources, send_ref, held, sems = refs[:6], refs[6], refs[7:13], refs[13]
    heads = send_ref.shape[0]
    rows = sources[0].shape[0]
    copies = fetch(sources, held, sems, (5, 4, 3, 0, 1, 2))
    for place in (5, 4, 3):
        copies[place].wait()
    for head in range(heads):
        cols = slice(head * HD, (head + 1) * HD)
        grads = held[3][:, cols]
        send_ref[head, 3 * rows : 4 * rows, :] = grads
        send_ref[head, 4 * rows :, :] = row_stats(
            grads, held[4][:, cols], held[5][head : head + 1, :]
        )
    for place in range(3):
        copies[place].wait()
        for head in range(heads):
            cols = slice(head * HD, (head + 1) * HD)
            send_ref[head, place * rows : (place + 1) * rows, :] = held[place][:, cols]


def near_head(query, keys, values, grads, stats):
    scores = dot(keys, query, NT)
    dprobs = dot(values, grads, NT)
    probs, centred = score_grads(scores, dprobs, stats.astype(jnp.float32))
    key_pos = lax.broadcasted_iota(jnp.int32, probs.shape, 0)
    query_pos = lax.broadcasted_iota(jnp.int32, probs.shape, 1)
    probs = jnp.where(key_pos <= query_pos, probs, 0.0)
    dscores = (probs * centred).astype(jnp.bfloat16)
    query_grad = dot(dscores, keys, TN) * SCALE
    key_grad = dot(dscores, query, NN) * SCALE
    return query_grad, key_grad, dot(probs.astype(jnp.bfloat16), grads, NN)


def near_kernel(*refs):
    sources, outs, stats_ref, held, sems = refs[:6], refs[6:9], refs[9], refs[10:16], refs[16]
    for copy in fetch(sources, held, sems, range(6)):
        copy.wait()
    for head in range(stats_ref.shape[0]):
        cols = slice(head * HD, (head + 1) * HD)
        parts = [held[place][:, cols] for place in range(4)]
        stats = row_stats(parts[3], held[4][:, cols], held[5][head : head + 1, :])
        stats_ref[head] = stats
        for ref, term in zip(outs, near_head(*parts, stats), strict=True):
            ref[:, cols] = term


class Head:
    def __init__(self, x_ref, out_ref, p_ref, ds_ref, kt_ref, stats_ref):
        self.x, self.out, self.p, self.ds, self.kt, self.stats = x_ref, out_ref, p_ref, ds_ref, kt_ref, stats_ref
        self.rows = out_ref.shape[1] // 3
        self.tokens = x_ref.shape[0] * self.rows
        for start in range(0, self.tokens, self.rows):
            cols = slice(start, start + self.rows)
            stats = x_ref[start // self.rows, 4 * self.rows :, :].astype(jnp.float32)
            stats_ref[0:1, cols] = stats[0:1] * LOG2E
            stats_ref[1:2, cols] = stats[1:2] + stats[2:3]
            kt_ref[:, cols] = self.piece(1, start, self.rows).T

    def piece(self, place, start, count):
        rows = self.rows
        blocks = slice(start // rows, (start + count) // rows)
        return self.x[blocks, place * rows : (place + 1) * rows, :].reshape(count, HD)

    def put(self, place, start, value):
        rows = self.rows
        for step in range(value.shape[0] // rows):
            part = value[step * rows : (step + 1) * rows].astype(jnp.bfloat16)
            self.out[start // rows + step, place * rows : (place + 1) * rows, :] = part

    def tile(self, keys, values, key_start, start, count, masked=False):
        key_rows, cols = slice(key_start, key_start + keys.shape[0]), slice(start, start + count)
        scores = dot(keys, self.piece(0, start, count), NT)
        dprobs = dot(values, self.piece(3, start, count), NT)
        probs = jnp.exp2(scores * (SCALE * LOG2E) - self.stats[0:1, cols])
        if masked:
            key_pos = lax.broadcasted_iota(jnp.int32, probs.shape, 0)
            query_pos = lax.broadcasted_iota(jnp.int32, probs.shape, 1)
            probs = jnp.where(key_pos <= query_pos, probs, 0.0)
        dscores = probs * (dprobs - self.stats[1:2, cols])
        self.p[key_rows, cols] = probs.astype(jnp.bfloat16)
        self.ds[key_rows, cols] = dscores.astype(jnp.bfloat16)


def whole_head_kernel(*refs):
    head = Head(*refs)
    step, tokens = 2 * head.rows, head.tokens
    for first in range(0, tokens, step):
        keys, values = head.piece(1, first, step), head.piece(2, first, step)
        for start in range(first, tokens, step):
            head.tile(keys, values, first, start, step, masked=start == first)
        rest, part = tokens - first, slice(first, first + step)
        head.put(1, first, dot(head.ds[part, first:], head.piece(0, first, rest), NN) * SCALE)
        head.put(2, first, dot(head.p[part, first:], head.piece(3, first, rest), NN))
    for first in range(0, tokens, step):
        stop = first + step
        head.put(0, first, dot(head.kt[:, :stop], head.ds[:stop, first:stop], NN).T * SCALE)


def far_head_kernel(*refs):
    head = Head(*refs)
    rows, tokens = head.rows, head.tokens
    step = 2 * rows
    for first in range(0, tokens, step):
        second, stop = first + rows, first + step
        keys, values = head.piece(1, first, step), head.piece(2, first, step)
        head.tile(keys[:rows], values[:rows], first, second, rows)
        for start in range(stop, tokens, step):
            head.tile(keys, values, first, start, step)
        for place, source, factor, ref in ((1, 0, SCALE, head.ds), (2, 3, 1.0, head.p)):
            total = dot(ref[first:second, second:stop], head.piece(source, second, rows), NN)
            after = jnp.zeros_like(total)
            if stop < tokens:
                far = dot(ref[first:stop, stop:], head.piece(source, stop, tokens - stop), NN)
                total, after = total + far[:rows], far[rows:]
            head.put(place, first, total * factor)
            head.put(place, second, after * factor)
    for first in range(0, tokens, step):
        second, stop = first + rows, first + step
        total = dot(head.kt[:, first:second], head.ds[first:second, second:stop], NN)
        before = jnp.zeros_like(total)
        if first > 0:
            far = dot(head.kt[:, :first], head.ds[:first, first:stop], NN)
            before, total = far[:, :rows], total + far[:, rows:]
        head.put(0, first, before.T * SCALE)
        head.put(0, second, total.T * SCALE)


def unpack_kernel(recv_ref, *refs):
    outs, sems = refs[:3], refs[3]
    rows = outs[0].shape[0]
    for place, ref in enumerate(outs):
        for head in range(recv_ref.shape[0]):
            pltpu.make_async_copy(
                recv_ref.at[head, place * rows : (place + 1) * rows, :],
                ref.at[:, head * HD : (head + 1) * HD],
                sems.at[place],
            ).start()
    for place, ref in enumerate(outs):
        pltpu.make_async_copy(ref, ref, sems.at[place]).wait()


def unpack_add_kernel(recv_ref, *refs):
    near, outs, sums, sems = refs[:3], refs[3:6], refs[6:9], refs[9]
    rows = outs[0].shape[0]
    copies = []
    for place, (part, buffer, ref) in enumerate(zip(near, sums, outs, strict=True)):
        for head in range(recv_ref.shape[0]):
            cols = slice(head * HD, (head + 1) * HD)
            far = recv_ref[head, place * rows : (place + 1) * rows, :].astype(jnp.float32)
            buffer[:, cols] = (far + part[:, cols]).astype(jnp.bfloat16)
        copies.append(pltpu.make_async_copy(buffer, ref, sems.at[place]))
        copies[-1].start()
    for copy in copies:
        copy.wait()


def bf16(*shape):
    return jax.ShapeDtypeStruct(shape, jnp.bfloat16)


def f32(*shape):
    return jax.ShapeDtypeStruct(shape, jnp.float32)


def call(kernel, name, in_specs, out_specs, out_shape, scratch):
    def run(*operands):
        operands = [
            pltpu.with_memory_space_constraint(operand, pltpu.HBM) if spec is IN_HBM else operand
            for spec, operand in zip(in_specs, operands, strict=True)
        ]
        with jax.named_scope(name):
            return pl.pallas_call(
                kernel,
                out_shape=out_shape,
                in_specs=in_specs,
                out_specs=out_specs,
                scratch_shapes=scratch,
                compiler_params=pltpu.CompilerParams(vmem_limit_bytes=KERNEL_LIMIT),
            )(*operands)

    return run


def exchange(chunks):
    with jax.named_scope("exchange"):
        return lax.all_to_all(chunks, "ctx", 0, 0, tiled=True)


def local(*arguments):
    queries, keys, values, outputs, out_grad, log_norm = arguments
    rows, width = queries.shape
    heads = width // HD
    tokens = rows * lax.axis_size("ctx")
    everything = (queries, keys, values, out_grad, outputs, log_norm)
    held = [pltpu.VMEM(operand.shape, operand.dtype) for operand in everything]
    chunk = bf16(heads, 4 * rows + STATS, HD)
    result = (bf16(rows, width),) * 3
    copies = pltpu.SemaphoreType.DMA

    def head_grads(kernel, x):
        scratch = (
            pltpu.VMEM((tokens, tokens), jnp.bfloat16),
            pltpu.VMEM((tokens, tokens), jnp.bfloat16),
            pltpu.VMEM((HD, tokens), jnp.bfloat16),
            pltpu.VMEM((8, tokens), jnp.float32),
        )
        shape = bf16(heads, 3 * rows, HD)
        return call(kernel, "head_grads", [IN_VMEM], IN_VMEM, shape, scratch)(x)

    def goes_first():
        pack = call(pack_kernel, "pack", [IN_HBM] * 6, IN_VMEM, chunk, (*held, copies((6,))))
        back = exchange(head_grads(whole_head_kernel, exchange(pack(*everything))))
        unpack = call(unpack_kernel, "unpack", [IN_VMEM], (IN_HBM,) * 3, result, (copies((3,)),))
        return unpack(back)

    def goes_second():
        shapes = (*(f32(rows, width),) * 3, bf16(heads, STATS, HD))
        near = call(near_kernel, "near", [IN_HBM] * 6, (IN_VMEM,) * 4, shapes, (*held, copies((6,))))
        *terms, stats = near(*everything)
        with jax.named_scope("pack"):
            by_heads = [x.reshape(rows, heads, HD).transpose(1, 0, 2) for x in everything[:4]]
            send = jnp.concatenate((*by_heads, stats), axis=1)
        back = exchange(head_grads(far_head_kernel, exchange(send)))
        scratch = (*(pltpu.VMEM((rows, width), jnp.bfloat16),) * 3, copies((3,)))
        unpack = call(unpack_add_kernel, "unpack", [IN_VMEM] * 4, (IN_HBM,) * 3, result, scratch)
        return unpack(back, *terms)

    return lax.cond(lax.axis_index("doc") % 2 == 1, goes_first, goes_second)


def solution(mesh):
    tokens = P(("doc", "ctx"), None)
    in_specs = (tokens,) * 5 + (P(None, ("doc", "ctx")),)
    return jax.shard_map(
        local, mesh=mesh, in_specs=in_specs, out_specs=(tokens,) * 3, check_vma=False
    )
```

```python
import functools
import math

import jax
import jax.numpy as jnp
from jax import lax
from jax.experimental import pallas as pl
from jax.experimental.pallas import tpu as pltpu
from jax.sharding import PartitionSpec as P

HD = 128
SCALE = HD**-0.5
LOG2E = math.log2(math.e)
STATS = 16
KERNEL_LIMIT = 32 * 1024 * 1024

NT = (((1,), (1,)), ((), ()))
NN = (((1,), (0,)), ((), ()))
TN = (((0,), (0,)), ((), ()))

IN_HBM = pl.BlockSpec(memory_space=pltpu.HBM)
IN_VMEM = pl.BlockSpec(memory_space=pltpu.VMEM)


def dot(left, right, dims):
    return lax.dot_general(left, right, dims, preferred_element_type=jnp.float32)


def row_stats(grads, outs, lse):
    product = (grads.astype(jnp.float32) * outs.astype(jnp.float32)).T
    delta = jnp.sum(product, axis=0, keepdims=True)
    delta_high = delta.astype(jnp.bfloat16).astype(jnp.float32)
    which = lax.broadcasted_iota(jnp.int32, (STATS, delta.shape[1]), 0)
    stats = jnp.where(which == 1, delta_high, delta - delta_high)
    return jnp.where(which == 0, lse.astype(jnp.float32), stats).astype(jnp.bfloat16)


def score_grads(scores, dprobs, stats):
    probs = jnp.exp2(scores * (SCALE * LOG2E) - stats[0:1] * LOG2E)
    return probs, dprobs - stats[1:2] - stats[2:3]


def fetch(sources, held, sems, order):
    copies = [
        pltpu.make_async_copy(source, buffer, sems.at[place])
        for place, (source, buffer) in enumerate(zip(sources, held, strict=True))
    ]
    for place in order:
        copies[place].start()
    return copies


def pack_kernel(*refs):
    sources, send_ref, held, sems = refs[:6], refs[6], refs[7:13], refs[13]
    heads = send_ref.shape[0]
    rows = sources[0].shape[0]
    copies = fetch(sources, held, sems, (5, 4, 3, 0, 1, 2))
    for place in (5, 4, 3):
        copies[place].wait()
    for head in range(heads):
        cols = slice(head * HD, (head + 1) * HD)
        grads = held[3][:, cols]
        send_ref[head, 3 * rows : 4 * rows, :] = grads
        send_ref[head, 4 * rows :, :] = row_stats(
            grads, held[4][:, cols], held[5][head : head + 1, :]
        )
    for place in range(3):
        copies[place].wait()
        for head in range(heads):
            cols = slice(head * HD, (head + 1) * HD)
            send_ref[head, place * rows : (place + 1) * rows, :] = held[place][:, cols]


def near_head(query, keys, values, grads, stats):
    scores = dot(keys, query, NT)
    dprobs = dot(values, grads, NT)
    probs, centred = score_grads(scores, dprobs, stats.astype(jnp.float32))
    key_pos = lax.broadcasted_iota(jnp.int32, probs.shape, 0)
    query_pos = lax.broadcasted_iota(jnp.int32, probs.shape, 1)
    probs = jnp.where(key_pos <= query_pos, probs, 0.0)
    dscores = (probs * centred).astype(jnp.bfloat16)
    query_grad = dot(dscores, keys, TN) * SCALE
    key_grad = dot(dscores, query, NN) * SCALE
    return query_grad, key_grad, dot(probs.astype(jnp.bfloat16), grads, NN)


def near_kernel(*refs):
    sources, outs, stats_ref, held, sems = refs[:6], refs[6:9], refs[9], refs[10:16], refs[16]
    for copy in fetch(sources, held, sems, range(6)):
        copy.wait()
    for head in range(stats_ref.shape[0]):
        cols = slice(head * HD, (head + 1) * HD)
        parts = [held[place][:, cols] for place in range(4)]
        stats = row_stats(parts[3], held[4][:, cols], held[5][head : head + 1, :])
        stats_ref[head] = stats
        for ref, term in zip(outs, near_head(*parts, stats), strict=True):
            ref[:, cols] = term


class Head:
    def __init__(self, x_ref, out_ref, p_ref, ds_ref, qt_ref, gt_ref, lse_ref, delta_ref):
        self.x, self.out, self.p, self.ds, self.qt, self.gt = x_ref, out_ref, p_ref, ds_ref, qt_ref, gt_ref
        self.lse, self.delta = lse_ref, delta_ref
        self.rows = out_ref.shape[1] // 3
        self.tokens = x_ref.shape[0] * self.rows
        for start in range(0, self.tokens, self.rows):
            part = slice(start, start + self.rows)
            stats = x_ref[start // self.rows, 4 * self.rows :, :].astype(jnp.float32)
            for ref, row in ((lse_ref, stats[0:1] * LOG2E), (delta_ref, stats[1:2] + stats[2:3])):
                ref[part, :] = jnp.broadcast_to(row, (HD, self.rows)).T
            qt_ref[:, part] = self.piece(0, start, self.rows).T
            gt_ref[:, part] = self.piece(3, start, self.rows).T

    def piece(self, place, start, count):
        rows = self.rows
        blocks = slice(start // rows, (start + count) // rows)
        return self.x[blocks, place * rows : (place + 1) * rows, :].reshape(count, HD)

    def put(self, place, start, value):
        rows = self.rows
        for step in range(value.shape[0] // rows):
            part = value[step * rows : (step + 1) * rows].astype(jnp.bfloat16)
            self.out[start // rows + step, place * rows : (place + 1) * rows, :] = part

    def tile(self, query, grads, start, key_start, count, masked=False):
        part, cols = slice(start, start + query.shape[0]), slice(key_start, key_start + count)
        scores = dot(query, self.piece(1, key_start, count), NT)
        dprobs = dot(grads, self.piece(2, key_start, count), NT)
        lse = jnp.concatenate([self.lse[part, :]] * (count // HD), axis=1)
        delta = jnp.concatenate([self.delta[part, :]] * (count // HD), axis=1)
        probs = jnp.exp2(scores * (SCALE * LOG2E) - lse)
        if masked:
            query_pos = lax.broadcasted_iota(jnp.int32, probs.shape, 0)
            key_pos = lax.broadcasted_iota(jnp.int32, probs.shape, 1)
            probs = jnp.where(key_pos <= query_pos, probs, 0.0)
        dscores = probs * (dprobs - delta)
        self.p[part, cols] = probs.astype(jnp.bfloat16)
        self.ds[part, cols] = dscores.astype(jnp.bfloat16)


def whole_head_kernel(*refs):
    head = Head(*refs)
    step, tokens = 2 * head.rows, head.tokens
    for first in range(0, tokens, step):
        stop = first + step
        query, grads = head.piece(0, first, step), head.piece(3, first, step)
        for start in range(0, stop, step):
            head.tile(query, grads, first, start, step, masked=start == first)
        head.put(0, first, dot(head.ds[first:stop, :stop], head.piece(1, 0, stop), NN) * SCALE)
    for first in range(0, tokens, step):
        cols = slice(first, first + step)
        head.put(1, first, dot(head.qt[:, first:], head.ds[first:, cols], NN).T * SCALE)
        head.put(2, first, dot(head.gt[:, first:], head.p[first:, cols], NN).T)


def far_head_kernel(*refs):
    head = Head(*refs)
    rows, tokens = head.rows, head.tokens
    step = 2 * rows
    for first in range(0, tokens, step):
        second, stop = first + rows, first + step
        query, grads = head.piece(0, first, step), head.piece(3, first, step)
        for start in range(0, first, step):
            head.tile(query, grads, first, start, step)
        head.tile(query[rows:], grads[rows:], second, first, rows)
        total = dot(head.ds[second:stop, first:second], head.piece(1, first, rows), NN)
        before = jnp.zeros_like(total)
        if first > 0:
            far = dot(head.ds[first:stop, :first], head.piece(1, 0, first), NN)
            before, total = far[:rows], total + far[rows:]
        head.put(0, first, before * SCALE)
        head.put(0, second, total * SCALE)
    for first in range(0, tokens, step):
        second, stop = first + rows, first + step
        for place, ref, turned, factor in ((1, head.ds, head.qt, SCALE), (2, head.p, head.gt, 1.0)):
            total = dot(turned[:, second:stop], ref[second:stop, first:second], NN)
            after = jnp.zeros_like(total)
            if stop < tokens:
                far = dot(turned[:, stop:], ref[stop:, first:stop], NN)
                total, after = total + far[:, :rows], far[:, rows:]
            head.put(place, first, total.T * factor)
            head.put(place, second, after.T * factor)


def unpack_kernel(recv_ref, *refs):
    outs, sems = refs[:3], refs[3]
    rows = outs[0].shape[0]
    for place, ref in enumerate(outs):
        for head in range(recv_ref.shape[0]):
            pltpu.make_async_copy(
                recv_ref.at[head, place * rows : (place + 1) * rows, :],
                ref.at[:, head * HD : (head + 1) * HD],
                sems.at[place],
            ).start()
    for place, ref in enumerate(outs):
        pltpu.make_async_copy(ref, ref, sems.at[place]).wait()


def unpack_add_kernel(recv_ref, *refs):
    near, outs, sums, sems = refs[:3], refs[3:6], refs[6:9], refs[9]
    rows = outs[0].shape[0]
    copies = []
    for place, (part, buffer, ref) in enumerate(zip(near, sums, outs, strict=True)):
        for head in range(recv_ref.shape[0]):
            cols = slice(head * HD, (head + 1) * HD)
            far = recv_ref[head, place * rows : (place + 1) * rows, :].astype(jnp.float32)
            buffer[:, cols] = (far + part[:, cols]).astype(jnp.bfloat16)
        copies.append(pltpu.make_async_copy(buffer, ref, sems.at[place]))
        copies[-1].start()
    for copy in copies:
        copy.wait()


def bf16(*shape):
    return jax.ShapeDtypeStruct(shape, jnp.bfloat16)


def f32(*shape):
    return jax.ShapeDtypeStruct(shape, jnp.float32)


def call(kernel, name, in_specs, out_specs, out_shape, scratch):
    def run(*operands):
        operands = [
            pltpu.with_memory_space_constraint(operand, pltpu.HBM) if spec is IN_HBM else operand
            for spec, operand in zip(in_specs, operands, strict=True)
        ]
        with jax.named_scope(name):
            return pl.pallas_call(
                kernel,
                out_shape=out_shape,
                in_specs=in_specs,
                out_specs=out_specs,
                scratch_shapes=scratch,
                compiler_params=pltpu.CompilerParams(vmem_limit_bytes=KERNEL_LIMIT),
            )(*operands)

    return run


def exchange(chunks):
    with jax.named_scope("exchange"):
        return lax.all_to_all(chunks, "ctx", 0, 0, tiled=True)


def local(*arguments):
    queries, keys, values, outputs, out_grad, log_norm = arguments
    rows, width = queries.shape
    heads = width // HD
    tokens = rows * lax.axis_size("ctx")
    everything = (queries, keys, values, out_grad, outputs, log_norm)
    held = [pltpu.VMEM(operand.shape, operand.dtype) for operand in everything]
    chunk = bf16(heads, 4 * rows + STATS, HD)
    result = (bf16(rows, width),) * 3
    copies = pltpu.SemaphoreType.DMA

    def head_grads(kernel, x):
        scratch = (
            pltpu.VMEM((tokens, tokens), jnp.bfloat16),
            pltpu.VMEM((tokens, tokens), jnp.bfloat16),
            pltpu.VMEM((HD, tokens), jnp.bfloat16),
            pltpu.VMEM((HD, tokens), jnp.bfloat16),
            pltpu.VMEM((tokens, HD), jnp.float32),
            pltpu.VMEM((tokens, HD), jnp.float32),
        )
        shape = bf16(heads, 3 * rows, HD)
        return call(kernel, "head_grads", [IN_VMEM], IN_VMEM, shape, scratch)(x)

    def goes_first():
        pack = call(pack_kernel, "pack", [IN_HBM] * 6, IN_VMEM, chunk, (*held, copies((6,))))
        back = exchange(head_grads(whole_head_kernel, exchange(pack(*everything))))
        unpack = call(unpack_kernel, "unpack", [IN_VMEM], (IN_HBM,) * 3, result, (copies((3,)),))
        return unpack(back)

    def goes_second():
        shapes = (*(f32(rows, width),) * 3, bf16(heads, STATS, HD))
        near = call(near_kernel, "near", [IN_HBM] * 6, (IN_VMEM,) * 4, shapes, (*held, copies((6,))))
        *terms, stats = near(*everything)
        with jax.named_scope("pack"):
            by_heads = [x.reshape(rows, heads, HD).transpose(1, 0, 2) for x in everything[:4]]
            send = jnp.concatenate((*by_heads, stats), axis=1)
        back = exchange(head_grads(far_head_kernel, exchange(send)))
        scratch = (*(pltpu.VMEM((rows, width), jnp.bfloat16),) * 3, copies((3,)))
        unpack = call(unpack_add_kernel, "unpack", [IN_VMEM] * 4, (IN_HBM,) * 3, result, scratch)
        return unpack(back, *terms)

    return lax.cond(lax.axis_index("doc") % 2 == 1, goes_first, goes_second)


def solution(mesh):
    tokens = P(("doc", "ctx"), None)
    in_specs = (tokens,) * 5 + (P(None, ("doc", "ctx")),)
    return jax.shard_map(
        local, mesh=mesh, in_specs=in_specs, out_specs=(tokens,) * 3, check_vma=False
    )
```

```python
import functools
import math

import jax
import jax.numpy as jnp
from jax import lax
from jax.experimental import pallas as pl
from jax.experimental.pallas import tpu as pltpu
from jax.sharding import PartitionSpec as P

HD = 128
SCALE = HD**-0.5
LOG2E = math.log2(math.e)
STATS = 16
KERNEL_LIMIT = 32 * 1024 * 1024

NT = (((1,), (1,)), ((), ()))
NN = (((1,), (0,)), ((), ()))
TN = (((0,), (0,)), ((), ()))

IN_HBM = pl.BlockSpec(memory_space=pltpu.HBM)
IN_VMEM = pl.BlockSpec(memory_space=pltpu.VMEM)


def dot(left, right, dims):
    return lax.dot_general(left, right, dims, preferred_element_type=jnp.float32)


def row_stats(grads, outs, lse):
    product = (grads.astype(jnp.float32) * outs.astype(jnp.float32)).T
    delta = jnp.sum(product, axis=0, keepdims=True)
    delta_high = delta.astype(jnp.bfloat16).astype(jnp.float32)
    which = lax.broadcasted_iota(jnp.int32, (STATS, delta.shape[1]), 0)
    stats = jnp.where(which == 1, delta_high, delta - delta_high)
    return jnp.where(which == 0, lse.astype(jnp.float32), stats).astype(jnp.bfloat16)


def score_grads(scores, dprobs, stats):
    probs = jnp.exp2(scores * (SCALE * LOG2E) - stats[0:1] * LOG2E)
    return probs, dprobs - stats[1:2] - stats[2:3]


def fetch(sources, held, sems, order):
    copies = [
        pltpu.make_async_copy(source, buffer, sems.at[place])
        for place, (source, buffer) in enumerate(zip(sources, held, strict=True))
    ]
    for place in order:
        copies[place].start()
    return copies


def pack_kernel(*refs):
    sources, send_ref, held, sems = refs[:6], refs[6], refs[7:13], refs[13]
    heads = send_ref.shape[0]
    rows = sources[0].shape[0]
    copies = fetch(sources, held, sems, (5, 4, 3, 0, 1, 2))
    for place in (5, 4, 3):
        copies[place].wait()
    for head in range(heads):
        cols = slice(head * HD, (head + 1) * HD)
        grads = held[3][:, cols]
        send_ref[head, 3 * rows : 4 * rows, :] = grads
        send_ref[head, 4 * rows :, :] = row_stats(
            grads, held[4][:, cols], held[5][head : head + 1, :]
        )
    for place in range(3):
        copies[place].wait()
        for head in range(heads):
            cols = slice(head * HD, (head + 1) * HD)
            send_ref[head, place * rows : (place + 1) * rows, :] = held[place][:, cols]


def near_head(query, keys, values, grads, stats):
    scores = dot(keys, query, NT)
    dprobs = dot(values, grads, NT)
    probs, centred = score_grads(scores, dprobs, stats.astype(jnp.float32))
    key_pos = lax.broadcasted_iota(jnp.int32, probs.shape, 0)
    query_pos = lax.broadcasted_iota(jnp.int32, probs.shape, 1)
    probs = jnp.where(key_pos <= query_pos, probs, 0.0)
    dscores = (probs * centred).astype(jnp.bfloat16)
    query_grad = dot(dscores, keys, TN) * SCALE
    key_grad = dot(dscores, query, NN) * SCALE
    return query_grad, key_grad, dot(probs.astype(jnp.bfloat16), grads, NN)


def near_kernel(*refs):
    sources, outs, stats_ref, held, sems = refs[:6], refs[6:9], refs[9], refs[10:16], refs[16]
    for copy in fetch(sources, held, sems, range(6)):
        copy.wait()
    for head in range(stats_ref.shape[0]):
        cols = slice(head * HD, (head + 1) * HD)
        parts = [held[place][:, cols] for place in range(4)]
        stats = row_stats(parts[3], held[4][:, cols], held[5][head : head + 1, :])
        stats_ref[head] = stats
        for ref, term in zip(outs, near_head(*parts, stats), strict=True):
            ref[:, cols] = term


class Head:
    def __init__(self, x_ref, out_ref, p_ref, ds_ref, qt_ref, gt_ref, lse_ref, delta_ref):
        self.x, self.out, self.p, self.ds, self.qt, self.gt = x_ref, out_ref, p_ref, ds_ref, qt_ref, gt_ref
        self.lse, self.delta = lse_ref, delta_ref
        self.rows = out_ref.shape[1] // 3
        self.tokens = x_ref.shape[0] * self.rows
        for start in range(0, self.tokens, self.rows):
            part = slice(start, start + self.rows)
            stats = x_ref[start // self.rows, 4 * self.rows :, :].astype(jnp.float32)
            for ref, row in ((lse_ref, stats[0:1] * LOG2E), (delta_ref, stats[1:2] + stats[2:3])):
                ref[part, :] = jnp.broadcast_to(row, (HD, self.rows)).T
            qt_ref[:, part] = self.piece(0, start, self.rows).T
            gt_ref[:, part] = self.piece(3, start, self.rows).T

    def piece(self, place, start, count):
        rows = self.rows
        blocks = slice(start // rows, (start + count) // rows)
        return self.x[blocks, place * rows : (place + 1) * rows, :].reshape(count, HD)

    def put(self, place, start, value):
        rows = self.rows
        for step in range(value.shape[0] // rows):
            part = value[step * rows : (step + 1) * rows].astype(jnp.bfloat16)
            self.out[start // rows + step, place * rows : (place + 1) * rows, :] = part

    def tile(self, query, grads, start, key_start, count, masked=False):
        part, cols = slice(start, start + query.shape[0]), slice(key_start, key_start + count)
        scores = dot(query, self.piece(1, key_start, count), NT)
        dprobs = dot(grads, self.piece(2, key_start, count), NT)
        lse = jnp.concatenate([self.lse[part, :]] * (count // HD), axis=1)
        delta = jnp.concatenate([self.delta[part, :]] * (count // HD), axis=1)
        probs = jnp.exp2(scores * (SCALE * LOG2E) - lse)
        if masked:
            query_pos = lax.broadcasted_iota(jnp.int32, probs.shape, 0)
            key_pos = lax.broadcasted_iota(jnp.int32, probs.shape, 1)
            probs = jnp.where(key_pos <= query_pos, probs, 0.0)
        dscores = probs * (dprobs - delta)
        self.p[part, cols] = probs.astype(jnp.bfloat16)
        self.ds[part, cols] = dscores.astype(jnp.bfloat16)


def last_to_first(tokens, step, tiles, sums):
    done = None
    for first in reversed(range(0, tokens, step)):
        tiles(first)
        if done is not None:
            sums(done)
        done = first
    sums(done)


def whole_head_kernel(*refs):
    head = Head(*refs)
    step = 2 * head.rows

    def tiles(first):
        query, grads = head.piece(0, first, step), head.piece(3, first, step)
        for start in range(0, first + step, step):
            head.tile(query, grads, first, start, step, masked=start == first)

    def sums(first):
        stop = first + step
        head.put(0, first, dot(head.ds[first:stop, :stop], head.piece(1, 0, stop), NN) * SCALE)
        head.put(1, first, dot(head.qt[:, first:], head.ds[first:, first:stop], NN).T * SCALE)
        head.put(2, first, dot(head.gt[:, first:], head.p[first:, first:stop], NN).T)

    last_to_first(head.tokens, step, tiles, sums)


def far_head_kernel(*refs):
    head = Head(*refs)
    rows, tokens = head.rows, head.tokens
    step = 2 * rows

    def tiles(first):
        query, grads = head.piece(0, first, step), head.piece(3, first, step)
        for start in range(0, first, step):
            head.tile(query, grads, first, start, step)
        head.tile(query[rows:], grads[rows:], first + rows, first, rows)

    def sums(first):
        second, stop = first + rows, first + step
        total = dot(head.ds[second:stop, first:second], head.piece(1, first, rows), NN)
        before = jnp.zeros_like(total)
        if first > 0:
            far = dot(head.ds[first:stop, :first], head.piece(1, 0, first), NN)
            before, total = far[:rows], total + far[rows:]
        head.put(0, first, before * SCALE)
        head.put(0, second, total * SCALE)
        for place, ref, turned, factor in ((1, head.ds, head.qt, SCALE), (2, head.p, head.gt, 1.0)):
            total = dot(turned[:, second:stop], ref[second:stop, first:second], NN)
            after = jnp.zeros_like(total)
            if stop < tokens:
                far = dot(turned[:, stop:], ref[stop:, first:stop], NN)
                total, after = total + far[:, :rows], far[:, rows:]
            head.put(place, first, total.T * factor)
            head.put(place, second, after.T * factor)

    last_to_first(tokens, step, tiles, sums)


def unpack_kernel(recv_ref, *refs):
    outs, sems = refs[:3], refs[3]
    rows = outs[0].shape[0]
    for place, ref in enumerate(outs):
        for head in range(recv_ref.shape[0]):
            pltpu.make_async_copy(
                recv_ref.at[head, place * rows : (place + 1) * rows, :],
                ref.at[:, head * HD : (head + 1) * HD],
                sems.at[place],
            ).start()
    for place, ref in enumerate(outs):
        pltpu.make_async_copy(ref, ref, sems.at[place]).wait()


def unpack_add_kernel(recv_ref, *refs):
    near, outs, sums, sems = refs[:3], refs[3:6], refs[6:9], refs[9]
    rows = outs[0].shape[0]
    copies = []
    for place, (part, buffer, ref) in enumerate(zip(near, sums, outs, strict=True)):
        for head in range(recv_ref.shape[0]):
            cols = slice(head * HD, (head + 1) * HD)
            far = recv_ref[head, place * rows : (place + 1) * rows, :].astype(jnp.float32)
            buffer[:, cols] = (far + part[:, cols]).astype(jnp.bfloat16)
        copies.append(pltpu.make_async_copy(buffer, ref, sems.at[place]))
        copies[-1].start()
    for copy in copies:
        copy.wait()


def bf16(*shape):
    return jax.ShapeDtypeStruct(shape, jnp.bfloat16)


def f32(*shape):
    return jax.ShapeDtypeStruct(shape, jnp.float32)


def call(kernel, name, in_specs, out_specs, out_shape, scratch):
    def run(*operands):
        operands = [
            pltpu.with_memory_space_constraint(operand, pltpu.HBM) if spec is IN_HBM else operand
            for spec, operand in zip(in_specs, operands, strict=True)
        ]
        with jax.named_scope(name):
            return pl.pallas_call(
                kernel,
                out_shape=out_shape,
                in_specs=in_specs,
                out_specs=out_specs,
                scratch_shapes=scratch,
                compiler_params=pltpu.CompilerParams(vmem_limit_bytes=KERNEL_LIMIT),
            )(*operands)

    return run


def exchange(chunks):
    with jax.named_scope("exchange"):
        return lax.all_to_all(chunks, "ctx", 0, 0, tiled=True)


def local(*arguments):
    queries, keys, values, outputs, out_grad, log_norm = arguments
    rows, width = queries.shape
    heads = width // HD
    tokens = rows * lax.axis_size("ctx")
    everything = (queries, keys, values, out_grad, outputs, log_norm)
    held = [pltpu.VMEM(operand.shape, operand.dtype) for operand in everything]
    chunk = bf16(heads, 4 * rows + STATS, HD)
    result = (bf16(rows, width),) * 3
    copies = pltpu.SemaphoreType.DMA

    def head_grads(kernel, x):
        scratch = (
            pltpu.VMEM((tokens, tokens), jnp.bfloat16),
            pltpu.VMEM((tokens, tokens), jnp.bfloat16),
            pltpu.VMEM((HD, tokens), jnp.bfloat16),
            pltpu.VMEM((HD, tokens), jnp.bfloat16),
            pltpu.VMEM((tokens, HD), jnp.float32),
            pltpu.VMEM((tokens, HD), jnp.float32),
        )
        shape = bf16(heads, 3 * rows, HD)
        return call(kernel, "head_grads", [IN_VMEM], IN_VMEM, shape, scratch)(x)

    def goes_first():
        pack = call(pack_kernel, "pack", [IN_HBM] * 6, IN_VMEM, chunk, (*held, copies((6,))))
        back = exchange(head_grads(whole_head_kernel, exchange(pack(*everything))))
        unpack = call(unpack_kernel, "unpack", [IN_VMEM], (IN_HBM,) * 3, result, (copies((3,)),))
        return unpack(back)

    def goes_second():
        shapes = (*(f32(rows, width),) * 3, bf16(heads, STATS, HD))
        near = call(near_kernel, "near", [IN_HBM] * 6, (IN_VMEM,) * 4, shapes, (*held, copies((6,))))
        *terms, stats = near(*everything)
        with jax.named_scope("pack"):
            by_heads = [x.reshape(rows, heads, HD).transpose(1, 0, 2) for x in everything[:4]]
            send = jnp.concatenate((*by_heads, stats), axis=1)
        back = exchange(head_grads(far_head_kernel, exchange(send)))
        scratch = (*(pltpu.VMEM((rows, width), jnp.bfloat16),) * 3, copies((3,)))
        unpack = call(unpack_add_kernel, "unpack", [IN_VMEM] * 4, (IN_HBM,) * 3, result, scratch)
        return unpack(back, *terms)

    return lax.cond(lax.axis_index("doc") % 2 == 1, goes_first, goes_second)


def solution(mesh):
    tokens = P(("doc", "ctx"), None)
    in_specs = (tokens,) * 5 + (P(None, ("doc", "ctx")),)
    return jax.shard_map(
        local, mesh=mesh, in_specs=in_specs, out_specs=(tokens,) * 3, check_vma=False
    )
```

```python
import functools
import math

import jax
import jax.numpy as jnp
from jax import lax
from jax.experimental import pallas as pl
from jax.experimental.pallas import tpu as pltpu
from jax.sharding import PartitionSpec as P

HD = 128
SCALE = HD**-0.5
LOG2E = math.log2(math.e)
GROUP = 8
KERNEL_LIMIT = 32 * 1024 * 1024

NT = (((1,), (1,)), ((), ()))
NN = (((1,), (0,)), ((), ()))
TN = (((0,), (0,)), ((), ()))

IN_HBM = pl.BlockSpec(memory_space=pltpu.HBM)
IN_VMEM = pl.BlockSpec(memory_space=pltpu.VMEM)


def dot(left, right, dims):
    return lax.dot_general(left, right, dims, preferred_element_type=jnp.float32)


def row_stats(grads, outs, lse):
    product = (grads.astype(jnp.float32) * outs.astype(jnp.float32)).T
    delta = jnp.sum(product, axis=0, keepdims=True)
    delta_high = delta.astype(jnp.bfloat16).astype(jnp.float32)
    which = lax.broadcasted_iota(jnp.int32, (GROUP, delta.shape[1]), 0)
    stats = jnp.where(which == 1, delta_high, delta - delta_high)
    return jnp.where(which == 0, lse.astype(jnp.float32), stats).astype(jnp.bfloat16)


def score_grads(scores, dprobs, stats):
    probs = jnp.exp2(scores * (SCALE * LOG2E) - stats[0:1] * LOG2E)
    return probs, dprobs - stats[1:2] - stats[2:3]


def put_rows(send_ref, head, place, value):
    count = value.shape[0] // GROUP
    send_ref[head, place * count : (place + 1) * count] = value.reshape(count, GROUP, HD)


def fetch(sources, held, sems, order):
    copies = [
        pltpu.make_async_copy(source, buffer, sems.at[place])
        for place, (source, buffer) in enumerate(zip(sources, held, strict=True))
    ]
    for place in order:
        copies[place].start()
    return copies


def pack_kernel(*refs):
    sources, send_ref, held, sems = refs[:6], refs[6], refs[7:13], refs[13]
    heads = send_ref.shape[0]
    rows = sources[0].shape[0]
    copies = fetch(sources, held, sems, (5, 4, 3, 0, 1, 2))
    for place in (5, 4, 3):
        copies[place].wait()
    for head in range(heads):
        cols = slice(head * HD, (head + 1) * HD)
        grads = held[3][:, cols]
        put_rows(send_ref, head, 3, grads)
        send_ref[head, 4 * rows // GROUP] = row_stats(
            grads, held[4][:, cols], held[5][head : head + 1, :]
        )
    for place in range(3):
        copies[place].wait()
        for head in range(heads):
            cols = slice(head * HD, (head + 1) * HD)
            put_rows(send_ref, head, place, held[place][:, cols])


def near_head(query, keys, values, grads, stats):
    scores = dot(keys, query, NT)
    dprobs = dot(values, grads, NT)
    probs, centred = score_grads(scores, dprobs, stats.astype(jnp.float32))
    key_pos = lax.broadcasted_iota(jnp.int32, probs.shape, 0)
    query_pos = lax.broadcasted_iota(jnp.int32, probs.shape, 1)
    probs = jnp.where(key_pos <= query_pos, probs, 0.0)
    dscores = (probs * centred).astype(jnp.bfloat16)
    query_grad = dot(dscores, keys, TN) * SCALE
    key_grad = dot(dscores, query, NN) * SCALE
    return query_grad, key_grad, dot(probs.astype(jnp.bfloat16), grads, NN)


def near_kernel(*refs):
    sources, outs, stats_ref, held, sems = refs[:6], refs[6:9], refs[9], refs[10:16], refs[16]
    for copy in fetch(sources, held, sems, range(6)):
        copy.wait()
    for head in range(stats_ref.shape[0]):
        cols = slice(head * HD, (head + 1) * HD)
        parts = [held[place][:, cols] for place in range(4)]
        stats = row_stats(parts[3], held[4][:, cols], held[5][head : head + 1, :])
        stats_ref[head] = stats
        for ref, term in zip(outs, near_head(*parts, stats), strict=True):
            ref[:, cols] = term


class Head:
    def __init__(self, x_ref, out_ref, p_ref, ds_ref, qt_ref, gt_ref, lse_ref, delta_ref):
        self.x, self.out, self.p, self.ds, self.qt, self.gt = x_ref, out_ref, p_ref, ds_ref, qt_ref, gt_ref
        self.lse, self.delta = lse_ref, delta_ref
        self.rows = out_ref.shape[1] // 3
        self.tokens = x_ref.shape[0] * self.rows
        for start in range(0, self.tokens, self.rows):
            part = slice(start, start + self.rows)
            stats = x_ref[start // self.rows, 4 * self.rows // GROUP].astype(jnp.float32)
            for ref, row in ((lse_ref, stats[0:1] * LOG2E), (delta_ref, stats[1:2] + stats[2:3])):
                ref[part, :] = jnp.broadcast_to(row, (HD, self.rows)).T
            qt_ref[:, part] = self.piece(0, start, self.rows).T
            gt_ref[:, part] = self.piece(3, start, self.rows).T

    def piece(self, place, start, count):
        blocks = slice(start // self.rows, (start + count) // self.rows)
        groups = self.rows // GROUP
        return self.x[blocks, place * groups : (place + 1) * groups].reshape(count, HD)

    def put(self, place, start, value):
        rows = self.rows
        for step in range(value.shape[0] // rows):
            part = value[step * rows : (step + 1) * rows].astype(jnp.bfloat16)
            self.out[start // rows + step, place * rows : (place + 1) * rows, :] = part

    def tile(self, query, grads, start, key_start, count, masked=False):
        part, cols = slice(start, start + query.shape[0]), slice(key_start, key_start + count)
        scores = dot(query, self.piece(1, key_start, count), NT)
        dprobs = dot(grads, self.piece(2, key_start, count), NT)
        lse = jnp.concatenate([self.lse[part, :]] * (count // HD), axis=1)
        delta = jnp.concatenate([self.delta[part, :]] * (count // HD), axis=1)
        probs = jnp.exp2(scores * (SCALE * LOG2E) - lse)
        if masked:
            query_pos = lax.broadcasted_iota(jnp.int32, probs.shape, 0)
            key_pos = lax.broadcasted_iota(jnp.int32, probs.shape, 1)
            probs = jnp.where(key_pos <= query_pos, probs, 0.0)
        dscores = probs * (dprobs - delta)
        self.p[part, cols] = probs.astype(jnp.bfloat16)
        self.ds[part, cols] = dscores.astype(jnp.bfloat16)


def last_to_first(tokens, step, tiles, sums):
    done = None
    for first in reversed(range(0, tokens, step)):
        tiles(first)
        if done is not None:
            sums(done)
        done = first
    sums(done)


def whole_head_kernel(*refs):
    head = Head(*refs)
    step = 2 * head.rows

    def tiles(first):
        query, grads = head.piece(0, first, step), head.piece(3, first, step)
        for start in range(0, first + step, step):
            head.tile(query, grads, first, start, step, masked=start == first)

    def sums(first):
        stop = first + step
        head.put(0, first, dot(head.ds[first:stop, :stop], head.piece(1, 0, stop), NN) * SCALE)
        head.put(1, first, dot(head.qt[:, first:], head.ds[first:, first:stop], NN).T * SCALE)
        head.put(2, first, dot(head.gt[:, first:], head.p[first:, first:stop], NN).T)

    last_to_first(head.tokens, step, tiles, sums)


def far_head_kernel(*refs):
    head = Head(*refs)
    rows, tokens = head.rows, head.tokens
    step = 2 * rows

    def tiles(first):
        query, grads = head.piece(0, first, step), head.piece(3, first, step)
        for start in range(0, first, step):
            head.tile(query, grads, first, start, step)
        head.tile(query[rows:], grads[rows:], first + rows, first, rows)

    def sums(first):
        second, stop = first + rows, first + step
        total = dot(head.ds[second:stop, first:second], head.piece(1, first, rows), NN)
        before = jnp.zeros_like(total)
        if first > 0:
            far = dot(head.ds[first:stop, :first], head.piece(1, 0, first), NN)
            before, total = far[:rows], total + far[rows:]
        head.put(0, first, before * SCALE)
        head.put(0, second, total * SCALE)
        for place, ref, turned, factor in ((1, head.ds, head.qt, SCALE), (2, head.p, head.gt, 1.0)):
            total = dot(turned[:, second:stop], ref[second:stop, first:second], NN)
            after = jnp.zeros_like(total)
            if stop < tokens:
                far = dot(turned[:, stop:], ref[stop:, first:stop], NN)
                total, after = total + far[:, :rows], far[:, rows:]
            head.put(place, first, total.T * factor)
            head.put(place, second, after.T * factor)

    last_to_first(tokens, step, tiles, sums)


def unpack_kernel(recv_ref, *refs):
    outs, sems = refs[:3], refs[3]
    rows = outs[0].shape[0]
    for place, ref in enumerate(outs):
        for head in range(recv_ref.shape[0]):
            pltpu.make_async_copy(
                recv_ref.at[head, place * rows : (place + 1) * rows, :],
                ref.at[:, head * HD : (head + 1) * HD],
                sems.at[place],
            ).start()
    for place, ref in enumerate(outs):
        pltpu.make_async_copy(ref, ref, sems.at[place]).wait()


def unpack_add_kernel(recv_ref, *refs):
    near, outs, sums, sems = refs[:3], refs[3:6], refs[6:9], refs[9]
    rows = outs[0].shape[0]
    copies = []
    for place, (part, buffer, ref) in enumerate(zip(near, sums, outs, strict=True)):
        for head in range(recv_ref.shape[0]):
            cols = slice(head * HD, (head + 1) * HD)
            far = recv_ref[head, place * rows : (place + 1) * rows, :].astype(jnp.float32)
            buffer[:, cols] = (far + part[:, cols]).astype(jnp.bfloat16)
        copies.append(pltpu.make_async_copy(buffer, ref, sems.at[place]))
        copies[-1].start()
    for copy in copies:
        copy.wait()


def bf16(*shape):
    return jax.ShapeDtypeStruct(shape, jnp.bfloat16)


def f32(*shape):
    return jax.ShapeDtypeStruct(shape, jnp.float32)


def call(kernel, name, in_specs, out_specs, out_shape, scratch):
    def run(*operands):
        operands = [
            pltpu.with_memory_space_constraint(operand, pltpu.HBM) if spec is IN_HBM else operand
            for spec, operand in zip(in_specs, operands, strict=True)
        ]
        with jax.named_scope(name):
            return pl.pallas_call(
                kernel,
                out_shape=out_shape,
                in_specs=in_specs,
                out_specs=out_specs,
                scratch_shapes=scratch,
                compiler_params=pltpu.CompilerParams(vmem_limit_bytes=KERNEL_LIMIT),
            )(*operands)

    return run


def exchange(chunks):
    with jax.named_scope("exchange"):
        return lax.all_to_all(chunks, "ctx", 0, 0, tiled=True)


def local(*arguments):
    queries, keys, values, outputs, out_grad, log_norm = arguments
    rows, width = queries.shape
    heads = width // HD
    tokens = rows * lax.axis_size("ctx")
    everything = (queries, keys, values, out_grad, outputs, log_norm)
    held = [pltpu.VMEM(operand.shape, operand.dtype) for operand in everything]
    chunk = bf16(heads, 4 * rows // GROUP + 1, GROUP, HD)
    result = (bf16(rows, width),) * 3
    copies = pltpu.SemaphoreType.DMA

    def head_grads(kernel, x):
        scratch = (
            pltpu.VMEM((tokens, tokens), jnp.bfloat16),
            pltpu.VMEM((tokens, tokens), jnp.bfloat16),
            pltpu.VMEM((HD, tokens), jnp.bfloat16),
            pltpu.VMEM((HD, tokens), jnp.bfloat16),
            pltpu.VMEM((tokens, HD), jnp.float32),
            pltpu.VMEM((tokens, HD), jnp.float32),
        )
        shape = bf16(heads, 3 * rows, HD)
        return call(kernel, "head_grads", [IN_VMEM], IN_VMEM, shape, scratch)(x)

    def goes_first():
        pack = call(pack_kernel, "pack", [IN_HBM] * 6, IN_VMEM, chunk, (*held, copies((6,))))
        back = exchange(head_grads(whole_head_kernel, exchange(pack(*everything))))
        unpack = call(unpack_kernel, "unpack", [IN_VMEM], (IN_HBM,) * 3, result, (copies((3,)),))
        return unpack(back)

    def goes_second():
        shapes = (*(f32(rows, width),) * 3, bf16(heads, GROUP, HD))
        near = call(near_kernel, "near", [IN_HBM] * 6, (IN_VMEM,) * 4, shapes, (*held, copies((6,))))
        *terms, stats = near(*everything)
        with jax.named_scope("pack"):
            by_heads = [x.reshape(rows, heads, HD).transpose(1, 0, 2) for x in everything[:4]]
            send = jnp.concatenate((*by_heads, stats), axis=1).reshape(chunk.shape)
        back = exchange(head_grads(far_head_kernel, exchange(send)))
        scratch = (*(pltpu.VMEM((rows, width), jnp.bfloat16),) * 3, copies((3,)))
        unpack = call(unpack_add_kernel, "unpack", [IN_VMEM] * 4, (IN_HBM,) * 3, result, scratch)
        return unpack(back, *terms)

    return lax.cond(lax.axis_index("doc") % 2 == 1, goes_first, goes_second)


def solution(mesh):
    tokens = P(("doc", "ctx"), None)
    in_specs = (tokens,) * 5 + (P(None, ("doc", "ctx")),)
    return jax.shard_map(
        local, mesh=mesh, in_specs=in_specs, out_specs=(tokens,) * 3, check_vma=False
    )
```

```python
import functools
import math

import jax
import jax.numpy as jnp
from jax import lax
from jax.experimental import pallas as pl
from jax.experimental.pallas import tpu as pltpu
from jax.sharding import PartitionSpec as P

HD = 128
SCALE = HD**-0.5
LOG2E = math.log2(math.e)
GROUP = 8
KERNEL_LIMIT = 32 * 1024 * 1024

NT = (((1,), (1,)), ((), ()))
NN = (((1,), (0,)), ((), ()))
TN = (((0,), (0,)), ((), ()))

IN_HBM = pl.BlockSpec(memory_space=pltpu.HBM)
IN_VMEM = pl.BlockSpec(memory_space=pltpu.VMEM)


def dot(left, right, dims):
    return lax.dot_general(left, right, dims, preferred_element_type=jnp.float32)


def row_stats(grads, outs, lse):
    product = (grads.astype(jnp.float32) * outs.astype(jnp.float32)).T
    delta = jnp.sum(product, axis=0, keepdims=True)
    delta_high = delta.astype(jnp.bfloat16).astype(jnp.float32)
    which = lax.broadcasted_iota(jnp.int32, (GROUP, delta.shape[1]), 0)
    stats = jnp.where(which == 1, delta_high, delta - delta_high)
    return jnp.where(which == 0, lse.astype(jnp.float32), stats).astype(jnp.bfloat16)


def score_grads(scores, dprobs, stats):
    probs = jnp.exp2(scores * (SCALE * LOG2E) - stats[0:1] * LOG2E)
    return probs, dprobs - stats[1:2] - stats[2:3]


def put_rows(send_ref, head, place, value):
    count = value.shape[0] // GROUP
    send_ref[head, place * count : (place + 1) * count] = value.reshape(count, GROUP, HD)


def fetch(sources, held, sems, order):
    copies = [
        pltpu.make_async_copy(source, buffer, sems.at[place])
        for place, (source, buffer) in enumerate(zip(sources, held, strict=True))
    ]
    for place in order:
        copies[place].start()
    return copies


def pack_kernel(*refs):
    sources, send_ref, held, sems = refs[:6], refs[6], refs[7:13], refs[13]
    heads = send_ref.shape[0]
    rows, width = sources[0].shape
    half = width // 2
    lse = pltpu.make_async_copy(sources[5], held[5], sems.at[0])
    lse.start()
    copies = {}
    for place in ((4, 3), (0,), (1,), (2,)):
        for start in (0, half):
            for which in place:
                cols = slice(start, start + half)
                copy = pltpu.make_async_copy(
                    sources[which].at[:, cols], held[which].at[:, cols], sems.at[len(copies) + 1]
                )
                copy.start()
                copies[which, start] = copy
    lse.wait()
    for start in (0, half):
        copies[4, start].wait()
        copies[3, start].wait()
        for head in range(start // HD, (start + half) // HD):
            cols = slice(head * HD, (head + 1) * HD)
            grads = held[3][:, cols]
            put_rows(send_ref, head, 3, grads)
            send_ref[head, 4 * rows // GROUP] = row_stats(
                grads, held[4][:, cols], held[5][head : head + 1, :]
            )
    for place in range(3):
        for start in (0, half):
            copies[place, start].wait()
            for head in range(start // HD, (start + half) // HD):
                cols = slice(head * HD, (head + 1) * HD)
                put_rows(send_ref, head, place, held[place][:, cols])


def near_head(query, keys, values, grads, stats):
    scores = dot(keys, query, NT)
    dprobs = dot(values, grads, NT)
    probs, centred = score_grads(scores, dprobs, stats.astype(jnp.float32))
    key_pos = lax.broadcasted_iota(jnp.int32, probs.shape, 0)
    query_pos = lax.broadcasted_iota(jnp.int32, probs.shape, 1)
    probs = jnp.where(key_pos <= query_pos, probs, 0.0)
    dscores = (probs * centred).astype(jnp.bfloat16)
    query_grad = dot(dscores, keys, TN) * SCALE
    key_grad = dot(dscores, query, NN) * SCALE
    return query_grad, key_grad, dot(probs.astype(jnp.bfloat16), grads, NN)


def near_kernel(*refs):
    sources, outs, stats_ref, held, sems = refs[:6], refs[6:9], refs[9], refs[10:16], refs[16]
    for copy in fetch(sources, held, sems, range(6)):
        copy.wait()
    for head in range(stats_ref.shape[0]):
        cols = slice(head * HD, (head + 1) * HD)
        parts = [held[place][:, cols] for place in range(4)]
        stats = row_stats(parts[3], held[4][:, cols], held[5][head : head + 1, :])
        stats_ref[head] = stats
        for ref, term in zip(outs, near_head(*parts, stats), strict=True):
            ref[:, cols] = term


class Head:
    def __init__(self, x_ref, out_ref, p_ref, ds_ref, qt_ref, gt_ref, lse_ref, delta_ref):
        self.x, self.out, self.p, self.ds, self.qt, self.gt = x_ref, out_ref, p_ref, ds_ref, qt_ref, gt_ref
        self.lse, self.delta = lse_ref, delta_ref
        self.rows = out_ref.shape[1] // 3
        self.tokens = x_ref.shape[0] * self.rows
        for start in range(0, self.tokens, self.rows):
            part = slice(start, start + self.rows)
            stats = x_ref[start // self.rows, 4 * self.rows // GROUP].astype(jnp.float32)
            for ref, row in ((lse_ref, stats[0:1] * LOG2E), (delta_ref, stats[1:2] + stats[2:3])):
                ref[part, :] = jnp.broadcast_to(row, (HD, self.rows)).T
            qt_ref[:, part] = self.piece(0, start, self.rows).T
            gt_ref[:, part] = self.piece(3, start, self.rows).T

    def piece(self, place, start, count):
        blocks = slice(start // self.rows, (start + count) // self.rows)
        groups = self.rows // GROUP
        return self.x[blocks, place * groups : (place + 1) * groups].reshape(count, HD)

    def put(self, place, start, value):
        rows = self.rows
        for step in range(value.shape[0] // rows):
            part = value[step * rows : (step + 1) * rows].astype(jnp.bfloat16)
            self.out[start // rows + step, place * rows : (place + 1) * rows, :] = part

    def tile(self, query, grads, start, key_start, count, masked=False):
        part, cols = slice(start, start + query.shape[0]), slice(key_start, key_start + count)
        scores = dot(query, self.piece(1, key_start, count), NT)
        dprobs = dot(grads, self.piece(2, key_start, count), NT)
        lse = jnp.concatenate([self.lse[part, :]] * (count // HD), axis=1)
        delta = jnp.concatenate([self.delta[part, :]] * (count // HD), axis=1)
        probs = jnp.exp2(scores * (SCALE * LOG2E) - lse)
        if masked:
            query_pos = lax.broadcasted_iota(jnp.int32, probs.shape, 0)
            key_pos = lax.broadcasted_iota(jnp.int32, probs.shape, 1)
            probs = jnp.where(key_pos <= query_pos, probs, 0.0)
        dscores = probs * (dprobs - delta)
        self.p[part, cols] = probs.astype(jnp.bfloat16)
        self.ds[part, cols] = dscores.astype(jnp.bfloat16)


def last_to_first(tokens, step, tiles, sums):
    done = None
    for first in reversed(range(0, tokens, step)):
        tiles(first)
        if done is not None:
            sums(done)
        done = first
    sums(done)


def whole_head_kernel(*refs):
    head = Head(*refs)
    step = 2 * head.rows

    def tiles(first):
        query, grads = head.piece(0, first, step), head.piece(3, first, step)
        for start in range(0, first + step, step):
            head.tile(query, grads, first, start, step, masked=start == first)

    def sums(first):
        stop = first + step
        head.put(0, first, dot(head.ds[first:stop, :stop], head.piece(1, 0, stop), NN) * SCALE)
        head.put(1, first, dot(head.qt[:, first:], head.ds[first:, first:stop], NN).T * SCALE)
        head.put(2, first, dot(head.gt[:, first:], head.p[first:, first:stop], NN).T)

    last_to_first(head.tokens, step, tiles, sums)


def far_head_kernel(*refs):
    head = Head(*refs)
    rows, tokens = head.rows, head.tokens
    step = 2 * rows

    def tiles(first):
        query, grads = head.piece(0, first, step), head.piece(3, first, step)
        for start in range(0, first, step):
            head.tile(query, grads, first, start, step)
        head.tile(query[rows:], grads[rows:], first + rows, first, rows)

    def sums(first):
        second, stop = first + rows, first + step
        total = dot(head.ds[second:stop, first:second], head.piece(1, first, rows), NN)
        before = jnp.zeros_like(total)
        if first > 0:
            far = dot(head.ds[first:stop, :first], head.piece(1, 0, first), NN)
            before, total = far[:rows], total + far[rows:]
        head.put(0, first, before * SCALE)
        head.put(0, second, total * SCALE)
        for place, ref, turned, factor in ((1, head.ds, head.qt, SCALE), (2, head.p, head.gt, 1.0)):
            total = dot(turned[:, second:stop], ref[second:stop, first:second], NN)
            after = jnp.zeros_like(total)
            if stop < tokens:
                far = dot(turned[:, stop:], ref[stop:, first:stop], NN)
                total, after = total + far[:, :rows], far[:, rows:]
            head.put(place, first, total.T * factor)
            head.put(place, second, after.T * factor)

    last_to_first(tokens, step, tiles, sums)


def unpack_kernel(recv_ref, *refs):
    outs, sems = refs[:3], refs[3]
    rows = outs[0].shape[0]
    for place, ref in enumerate(outs):
        for head in range(recv_ref.shape[0]):
            pltpu.make_async_copy(
                recv_ref.at[head, place * rows : (place + 1) * rows, :],
                ref.at[:, head * HD : (head + 1) * HD],
                sems.at[place],
            ).start()
    for place, ref in enumerate(outs):
        pltpu.make_async_copy(ref, ref, sems.at[place]).wait()


def unpack_add_kernel(recv_ref, *refs):
    near, outs, sums, sems = refs[:3], refs[3:6], refs[6:9], refs[9]
    rows, width = outs[0].shape
    half = width // 2
    copies = []
    for place, (part, buffer, ref) in enumerate(zip(near, sums, outs, strict=True)):
        for start in range(0, width, half):
            for head in range(start // HD, (start + half) // HD):
                cols = slice(head * HD, (head + 1) * HD)
                far = recv_ref[head, place * rows : (place + 1) * rows, :].astype(jnp.float32)
                buffer[:, cols] = (far + part[:, cols]).astype(jnp.bfloat16)
            cols = slice(start, start + half)
            copies.append(
                pltpu.make_async_copy(buffer.at[:, cols], ref.at[:, cols], sems.at[len(copies)])
            )
            copies[-1].start()
    for copy in copies:
        copy.wait()


def bf16(*shape):
    return jax.ShapeDtypeStruct(shape, jnp.bfloat16)


def f32(*shape):
    return jax.ShapeDtypeStruct(shape, jnp.float32)


def call(kernel, name, in_specs, out_specs, out_shape, scratch):
    def run(*operands):
        operands = [
            pltpu.with_memory_space_constraint(operand, pltpu.HBM) if spec is IN_HBM else operand
            for spec, operand in zip(in_specs, operands, strict=True)
        ]
        with jax.named_scope(name):
            return pl.pallas_call(
                kernel,
                out_shape=out_shape,
                in_specs=in_specs,
                out_specs=out_specs,
                scratch_shapes=scratch,
                compiler_params=pltpu.CompilerParams(vmem_limit_bytes=KERNEL_LIMIT),
            )(*operands)

    return run


def exchange(chunks):
    with jax.named_scope("exchange"):
        return lax.all_to_all(chunks, "ctx", 0, 0, tiled=True)


def local(*arguments):
    queries, keys, values, outputs, out_grad, log_norm = arguments
    rows, width = queries.shape
    heads = width // HD
    tokens = rows * lax.axis_size("ctx")
    everything = (queries, keys, values, out_grad, outputs, log_norm)
    held = [pltpu.VMEM(operand.shape, operand.dtype) for operand in everything]
    chunk = bf16(heads, 4 * rows // GROUP + 1, GROUP, HD)
    result = (bf16(rows, width),) * 3
    copies = pltpu.SemaphoreType.DMA

    def head_grads(kernel, x):
        scratch = (
            pltpu.VMEM((tokens, tokens), jnp.bfloat16),
            pltpu.VMEM((tokens, tokens), jnp.bfloat16),
            pltpu.VMEM((HD, tokens), jnp.bfloat16),
            pltpu.VMEM((HD, tokens), jnp.bfloat16),
            pltpu.VMEM((tokens, HD), jnp.float32),
            pltpu.VMEM((tokens, HD), jnp.float32),
        )
        shape = bf16(heads, 3 * rows, HD)
        return call(kernel, "head_grads", [IN_VMEM], IN_VMEM, shape, scratch)(x)

    def goes_first():
        pack = call(pack_kernel, "pack", [IN_HBM] * 6, IN_VMEM, chunk, (*held, copies((11,))))
        back = exchange(head_grads(whole_head_kernel, exchange(pack(*everything))))
        unpack = call(unpack_kernel, "unpack", [IN_VMEM], (IN_HBM,) * 3, result, (copies((3,)),))
        return unpack(back)

    def goes_second():
        shapes = (*(f32(rows, width),) * 3, bf16(heads, GROUP, HD))
        near = call(near_kernel, "near", [IN_HBM] * 6, (IN_VMEM,) * 4, shapes, (*held, copies((6,))))
        *terms, stats = near(*everything)
        with jax.named_scope("pack"):
            by_heads = [x.reshape(rows, heads, HD).transpose(1, 0, 2) for x in everything[:4]]
            send = jnp.concatenate((*by_heads, stats), axis=1).reshape(chunk.shape)
        back = exchange(head_grads(far_head_kernel, exchange(send)))
        scratch = (*(pltpu.VMEM((rows, width), jnp.bfloat16),) * 3, copies((6,)))
        unpack = call(unpack_add_kernel, "unpack", [IN_VMEM] * 4, (IN_HBM,) * 3, result, scratch)
        return unpack(back, *terms)

    return lax.cond(lax.axis_index("doc") % 2 == 1, goes_first, goes_second)


def solution(mesh):
    tokens = P(("doc", "ctx"), None)
    in_specs = (tokens,) * 5 + (P(None, ("doc", "ctx")),)
    return jax.shard_map(
        local, mesh=mesh, in_specs=in_specs, out_specs=(tokens,) * 3, check_vma=False
    )
```

```python
import functools
import math

import jax
import jax.numpy as jnp
from jax import lax
from jax.experimental import pallas as pl
from jax.experimental.pallas import tpu as pltpu
from jax.sharding import PartitionSpec as P

HD = 128
SCALE = HD**-0.5
LOG2E = math.log2(math.e)
GROUP = 8
KERNEL_LIMIT = 32 * 1024 * 1024

NT = (((1,), (1,)), ((), ()))
NN = (((1,), (0,)), ((), ()))
TN = (((0,), (0,)), ((), ()))

IN_HBM = pl.BlockSpec(memory_space=pltpu.HBM)
IN_VMEM = pl.BlockSpec(memory_space=pltpu.VMEM)


def dot(left, right, dims):
    return lax.dot_general(left, right, dims, preferred_element_type=jnp.float32)


def row_stats(grads, outs, lse):
    product = (grads.astype(jnp.float32) * outs.astype(jnp.float32)).T
    delta = jnp.sum(product, axis=0, keepdims=True)
    delta_high = delta.astype(jnp.bfloat16).astype(jnp.float32)
    which = lax.broadcasted_iota(jnp.int32, (GROUP, delta.shape[1]), 0)
    stats = jnp.where(which == 1, delta_high, delta - delta_high)
    return jnp.where(which == 0, lse.astype(jnp.float32), stats).astype(jnp.bfloat16)


def score_grads(scores, dprobs, stats):
    probs = jnp.exp2(scores * (SCALE * LOG2E) - stats[0:1] * LOG2E)
    return probs, dprobs - stats[1:2] - stats[2:3]


def put_rows(send_ref, head, place, value):
    count = value.shape[0] // GROUP
    send_ref[head, place * count : (place + 1) * count] = value.reshape(count, GROUP, HD)


def fetch(sources, held, sems, order):
    copies = [
        pltpu.make_async_copy(source, buffer, sems.at[place])
        for place, (source, buffer) in enumerate(zip(sources, held, strict=True))
    ]
    for place in order:
        copies[place].start()
    return copies


def pack_kernel(*refs):
    sources, send_ref, held, sems = refs[:6], refs[6], refs[7:13], refs[13]
    heads = send_ref.shape[0]
    rows, width = sources[0].shape
    half = width // 2
    lse = pltpu.make_async_copy(sources[5], held[5], sems.at[0])
    lse.start()
    copies = {}
    for place in ((4, 3), (0,), (1,), (2,)):
        for start in (0, half):
            for which in place:
                cols = slice(start, start + half)
                copy = pltpu.make_async_copy(
                    sources[which].at[:, cols], held[which].at[:, cols], sems.at[len(copies) + 1]
                )
                copy.start()
                copies[which, start] = copy
    lse.wait()
    for start in (0, half):
        copies[4, start].wait()
        copies[3, start].wait()
        for head in range(start // HD, (start + half) // HD):
            cols = slice(head * HD, (head + 1) * HD)
            grads = held[3][:, cols]
            put_rows(send_ref, head, 3, grads)
            send_ref[head, 4 * rows // GROUP] = row_stats(
                grads, held[4][:, cols], held[5][head : head + 1, :]
            )
    for place in range(3):
        for start in (0, half):
            copies[place, start].wait()
            for head in range(start // HD, (start + half) // HD):
                cols = slice(head * HD, (head + 1) * HD)
                put_rows(send_ref, head, place, held[place][:, cols])


def near_head(query, keys, values, grads, stats):
    scores = dot(keys, query, NT)
    dprobs = dot(values, grads, NT)
    probs, centred = score_grads(scores, dprobs, stats.astype(jnp.float32))
    key_pos = lax.broadcasted_iota(jnp.int32, probs.shape, 0)
    query_pos = lax.broadcasted_iota(jnp.int32, probs.shape, 1)
    probs = jnp.where(key_pos <= query_pos, probs, 0.0)
    dscores = (probs * centred).astype(jnp.bfloat16)
    query_grad = dot(dscores, keys, TN) * SCALE
    key_grad = dot(dscores, query, NN) * SCALE
    return query_grad, key_grad, dot(probs.astype(jnp.bfloat16), grads, NN)


def near_kernel(*refs):
    sources, outs, stats_ref, held, sems = refs[:6], refs[6:9], refs[9], refs[10:16], refs[16]
    for copy in fetch(sources, held, sems, range(6)):
        copy.wait()
    for head in range(stats_ref.shape[0]):
        cols = slice(head * HD, (head + 1) * HD)
        parts = [held[place][:, cols] for place in range(4)]
        stats = row_stats(parts[3], held[4][:, cols], held[5][head : head + 1, :])
        stats_ref[head] = stats
        for ref, term in zip(outs, near_head(*parts, stats), strict=True):
            ref[:, cols] = term


class Head:
    def __init__(self, x_ref, out_ref, p_ref, ds_ref, qt_ref, gt_ref, lse_ref, delta_ref):
        self.x, self.out, self.p, self.ds, self.qt, self.gt = x_ref, out_ref, p_ref, ds_ref, qt_ref, gt_ref
        self.lse, self.delta = lse_ref, delta_ref
        self.rows = out_ref.shape[1] // 3
        self.tokens = x_ref.shape[0] * self.rows
        for start in range(0, self.tokens, self.rows):
            part = slice(start, start + self.rows)
            stats = x_ref[start // self.rows, 4 * self.rows // GROUP].astype(jnp.float32)
            for ref, row in ((lse_ref, stats[0:1] * LOG2E), (delta_ref, stats[1:2] + stats[2:3])):
                ref[part, :] = jnp.broadcast_to(row, (HD, self.rows)).T
            qt_ref[:, part] = self.piece(0, start, self.rows).T
            gt_ref[:, part] = self.piece(3, start, self.rows).T

    def piece(self, place, start, count):
        blocks = slice(start // self.rows, (start + count) // self.rows)
        groups = self.rows // GROUP
        return self.x[blocks, place * groups : (place + 1) * groups].reshape(count, HD)

    def put(self, place, start, value):
        rows = self.rows
        for step in range(value.shape[0] // rows):
            part = value[step * rows : (step + 1) * rows].astype(jnp.bfloat16)
            self.out[start // rows + step, place * rows : (place + 1) * rows, :] = part

    def tile(self, query, grads, start, key_start, count, masked=False):
        part, cols = slice(start, start + query.shape[0]), slice(key_start, key_start + count)
        scores = dot(query, self.piece(1, key_start, count), NT)
        dprobs = dot(grads, self.piece(2, key_start, count), NT)
        lse = jnp.concatenate([self.lse[part, :]] * (count // HD), axis=1)
        delta = jnp.concatenate([self.delta[part, :]] * (count // HD), axis=1)
        probs = jnp.exp2(scores * (SCALE * LOG2E) - lse)
        if masked:
            query_pos = lax.broadcasted_iota(jnp.int32, probs.shape, 0)
            key_pos = lax.broadcasted_iota(jnp.int32, probs.shape, 1)
            probs = jnp.where(key_pos <= query_pos, probs, 0.0)
        dscores = probs * (dprobs - delta)
        self.p[part, cols] = probs.astype(jnp.bfloat16)
        self.ds[part, cols] = dscores.astype(jnp.bfloat16)


def last_to_first(tokens, step, tiles, sums):
    done = None
    for first in reversed(range(0, tokens, step)):
        tiles(first)
        if done is not None:
            sums(done)
        done = first
    sums(done)


def whole_head_kernel(*refs):
    head = Head(*refs)
    step = 2 * head.rows

    def tiles(first):
        query, grads = head.piece(0, first, step), head.piece(3, first, step)
        for start in range(0, first + step, step):
            head.tile(query, grads, first, start, step, masked=start == first)

    def sums(first):
        stop = first + step
        head.put(0, first, dot(head.ds[first:stop, :stop], head.piece(1, 0, stop), NN) * SCALE)
        head.put(1, first, dot(head.qt[:, first:], head.ds[first:, first:stop], NN).T * SCALE)
        head.put(2, first, dot(head.gt[:, first:], head.p[first:, first:stop], NN).T)

    last_to_first(head.tokens, step, tiles, sums)


def far_head_kernel(*refs):
    head = Head(*refs)
    rows, tokens = head.rows, head.tokens
    step = 2 * rows

    def tiles(first):
        query, grads = head.piece(0, first, step), head.piece(3, first, step)
        if first > 0:
            head.tile(query, grads, first, 0, first)
        head.tile(query[rows:], grads[rows:], first + rows, first, rows)

    def sums(first):
        second, stop = first + rows, first + step
        total = dot(head.ds[second:stop, first:second], head.piece(1, first, rows), NN)
        before = jnp.zeros_like(total)
        if first > 0:
            far = dot(head.ds[first:stop, :first], head.piece(1, 0, first), NN)
            before, total = far[:rows], total + far[rows:]
        head.put(0, first, before * SCALE)
        head.put(0, second, total * SCALE)
        for place, ref, turned, factor in ((1, head.ds, head.qt, SCALE), (2, head.p, head.gt, 1.0)):
            total = dot(turned[:, second:stop], ref[second:stop, first:second], NN)
            after = jnp.zeros_like(total)
            if stop < tokens:
                far = dot(turned[:, stop:], ref[stop:, first:stop], NN)
                total, after = total + far[:, :rows], far[:, rows:]
            head.put(place, first, total.T * factor)
            head.put(place, second, after.T * factor)

    last_to_first(tokens, step, tiles, sums)


def unpack_kernel(recv_ref, *refs):
    outs, sems = refs[:3], refs[3]
    rows = outs[0].shape[0]
    for place, ref in enumerate(outs):
        for head in range(recv_ref.shape[0]):
            pltpu.make_async_copy(
                recv_ref.at[head, place * rows : (place + 1) * rows, :],
                ref.at[:, head * HD : (head + 1) * HD],
                sems.at[place],
            ).start()
    for place, ref in enumerate(outs):
        pltpu.make_async_copy(ref, ref, sems.at[place]).wait()


def unpack_add_kernel(recv_ref, *refs):
    near, outs, sums, sems = refs[:3], refs[3:6], refs[6:9], refs[9]
    rows, width = outs[0].shape
    half = width // 2
    copies = []
    for place, (part, buffer, ref) in enumerate(zip(near, sums, outs, strict=True)):
        for start in range(0, width, half):
            for head in range(start // HD, (start + half) // HD):
                cols = slice(head * HD, (head + 1) * HD)
                far = recv_ref[head, place * rows : (place + 1) * rows, :].astype(jnp.float32)
                buffer[:, cols] = (far + part[:, cols]).astype(jnp.bfloat16)
            cols = slice(start, start + half)
            copies.append(
                pltpu.make_async_copy(buffer.at[:, cols], ref.at[:, cols], sems.at[len(copies)])
            )
            copies[-1].start()
    for copy in copies:
        copy.wait()


def bf16(*shape):
    return jax.ShapeDtypeStruct(shape, jnp.bfloat16)


def f32(*shape):
    return jax.ShapeDtypeStruct(shape, jnp.float32)


def call(kernel, name, in_specs, out_specs, out_shape, scratch):
    def run(*operands):
        operands = [
            pltpu.with_memory_space_constraint(operand, pltpu.HBM) if spec is IN_HBM else operand
            for spec, operand in zip(in_specs, operands, strict=True)
        ]
        with jax.named_scope(name):
            return pl.pallas_call(
                kernel,
                out_shape=out_shape,
                in_specs=in_specs,
                out_specs=out_specs,
                scratch_shapes=scratch,
                compiler_params=pltpu.CompilerParams(vmem_limit_bytes=KERNEL_LIMIT),
            )(*operands)

    return run


def exchange(chunks):
    with jax.named_scope("exchange"):
        return lax.all_to_all(chunks, "ctx", 0, 0, tiled=True)


def local(*arguments):
    queries, keys, values, outputs, out_grad, log_norm = arguments
    rows, width = queries.shape
    heads = width // HD
    tokens = rows * lax.axis_size("ctx")
    everything = (queries, keys, values, out_grad, outputs, log_norm)
    held = [pltpu.VMEM(operand.shape, operand.dtype) for operand in everything]
    chunk = bf16(heads, 4 * rows // GROUP + 1, GROUP, HD)
    result = (bf16(rows, width),) * 3
    copies = pltpu.SemaphoreType.DMA

    def head_grads(kernel, x):
        scratch = (
            pltpu.VMEM((tokens, tokens), jnp.bfloat16),
            pltpu.VMEM((tokens, tokens), jnp.bfloat16),
            pltpu.VMEM((HD, tokens), jnp.bfloat16),
            pltpu.VMEM((HD, tokens), jnp.bfloat16),
            pltpu.VMEM((tokens, HD), jnp.float32),
            pltpu.VMEM((tokens, HD), jnp.float32),
        )
        shape = bf16(heads, 3 * rows, HD)
        return call(kernel, "head_grads", [IN_VMEM], IN_VMEM, shape, scratch)(x)

    def goes_first():
        pack = call(pack_kernel, "pack", [IN_HBM] * 6, IN_VMEM, chunk, (*held, copies((11,))))
        back = exchange(head_grads(whole_head_kernel, exchange(pack(*everything))))
        unpack = call(unpack_kernel, "unpack", [IN_VMEM], (IN_HBM,) * 3, result, (copies((3,)),))
        return unpack(back)

    def goes_second():
        shapes = (*(f32(rows, width),) * 3, bf16(heads, GROUP, HD))
        near = call(near_kernel, "near", [IN_HBM] * 6, (IN_VMEM,) * 4, shapes, (*held, copies((6,))))
        *terms, stats = near(*everything)
        with jax.named_scope("pack"):
            by_heads = [x.reshape(rows, heads, HD).transpose(1, 0, 2) for x in everything[:4]]
            send = jnp.concatenate((*by_heads, stats), axis=1).reshape(chunk.shape)
        back = exchange(head_grads(far_head_kernel, exchange(send)))
        scratch = (*(pltpu.VMEM((rows, width), jnp.bfloat16),) * 3, copies((6,)))
        unpack = call(unpack_add_kernel, "unpack", [IN_VMEM] * 4, (IN_HBM,) * 3, result, scratch)
        return unpack(back, *terms)

    return lax.cond(lax.axis_index("doc") % 2 == 1, goes_first, goes_second)


def solution(mesh):
    tokens = P(("doc", "ctx"), None)
    in_specs = (tokens,) * 5 + (P(None, ("doc", "ctx")),)
    return jax.shard_map(
        local, mesh=mesh, in_specs=in_specs, out_specs=(tokens,) * 3, check_vma=False
    )
```
